32 devices in a mesh: ctx: 4 (over y, core), exp: 8 (over z, x).
Axes of the slice: x: 2, y: 2, z: 4, core: 2. Of those that a mesh axis runs over, the one named last changes fastest.
Arguments:
- hidden: bfloat16 [8, 512, 4096], P('exp', 'ctx'), may hold values from -6 to 6
- queries: bfloat16 [8, 512, 4096], P('exp', 'ctx'), may hold values from -4.5 to 4.5
- new_keys: bfloat16 [8, 512, 512], P('exp', 'ctx'), may hold values from -6 to 6
- new_values: bfloat16 [8, 512, 512], P('exp', 'ctx'), may hold values from -6 to 6
- cache_keys: bfloat16 [8, 512, 512], P('exp', 'ctx'), may hold values from -4.5 to 4.5
- cache_values: bfloat16 [8, 512, 512], P('exp', 'ctx'), may hold values from -6 to 6
- out_weight: bfloat16 [4096, 4096], P(('ctx', 'exp')), may hold values from -1.5 to 1.5
- norm_gain: bfloat16 [4096], replicated, may hold values from 0.099609375 to 1.8984375
- gate_proj: bfloat16 [32, 4096, 768], P(('ctx', 'exp')), may hold values from -0.09375 to 0.09375
- up_proj: bfloat16 [32, 4096, 768], P(('ctx', 'exp')), may hold values from -0.09375 to 0.09375
- down_proj: bfloat16 [32, 768, 4096], P(('ctx', 'exp')), may hold values from -0.21875 to 0.21875
- expert_ids: int32 [8, 512, 4], P('exp', 'ctx'), may hold values from 0 to 31, all different within a row; in each aligned block of 128 rows (0 to 127, 128 to 255, ..., all dimensions but the last counted through in order) at most 32 rows name the same one
- gate_fixed: int32 [8, 512, 4], P('exp', 'ctx'), may hold values from 1 to 65535
Outputs:
- after_attention: bfloat16 [8, 512, 4096], P('exp', 'ctx')
- layer_output: bfloat16 [8, 512, 4096], P('exp', 'ctx')
The draws below stay inside these ranges and needn't reach their ends.
Inputs may be any that keep to these rules, and one draw needn't show every extreme that they name: `expert_ids`: each row names 4 different experts. Within the rows of one device (aligned blocks of 128 rows, sequences taken in order) no expert is named more than 32 times, and in some blocks one expert is named exactly 32 times.
All inputs are finite; a program needn't handle non-finite values.
Results may differ from the reference program's by a relative error of at most 0.02.
Values may be sent and summed in bfloat16 or wider, within the bound.
No kernel may reach another device: no remote copies, remote signals or barrier semaphores. Data moves between devices by JAX's collectives and lax.ppermute only.
A program may use at most 128 MiB of HBM per device.

```python
import math
import jax
import jax.numpy as jnp
import numpy as np
from jax import lax

D = 4096
HQ = 32
KVH = 4
HD = 128
MOE_FF = 768
TOPK = 4
TOK_DEV = 128
SEQS = 8
WINDOW = 512
CACHE = 512
EXPERTS = 32
CAP = 32
N_CTX = 4
N_EXP = 8


def draw_queries(key, part):
    base = 1.5 * jax.random.normal(jax.random.fold_in(key, 1), (SEQS, WINDOW, HQ * HD), jnp.float32)
    return jnp.clip(base, -4.5, 4.5).astype(jnp.bfloat16)


def draw_cache_keys(key, part):
    base = jax.random.normal(jax.random.fold_in(key, 4), (SEQS, CACHE, KVH * HD), jnp.float32)
    return jnp.clip(base, -4.5, 4.5).astype(jnp.bfloat16)


def set_ends(result, own_key, low, top_value):
    extent = result.shape
    index_at = [jax.random.randint(jax.random.fold_in(own_key, axis), (), 0, extent[axis]) for axis in range(len(extent))]
    result = result.at[tuple(index_at)].set(low)
    longest = extent.index(max(extent))
    index_at[longest] = (index_at[longest] + 1) % extent[longest]
    return result.at[tuple(index_at)].set(top_value)


def block_levels(rng, dims, cuts, least, largest):
    gain, own = 1.0, jax.random.fold_in(rng, 6)
    for position, parts in cuts:
        heights = jnp.exp(jax.random.uniform(jax.random.fold_in(own, position), (parts,), jnp.float32, least / len(cuts), largest / len(cuts)))
        gain = gain * jnp.repeat(heights, dims[position] // parts).reshape([-1 if axis == position else 1 for axis in range(len(dims))])
    return gain


def routed_block(stream_key, own, number, rows, amount, top, reach, skew):
    sequence = jax.random.permutation(stream_key, amount)
    heavy_load, usual = portions_of(amount, rows * top, reach, skew, True), portions_of(amount, rows * top, reach, skew, False)
    places = jnp.arange(amount)

    def named(sizes, rotation):
        used = int((sizes > 0).sum())
        fixed = max(1, used // 4)
        shifted = fixed + (places - fixed + rotation * (used - fixed)) % max(1, amount - fixed)
        return jnp.zeros((amount,), jnp.int32).at[sequence[jnp.where(places < fixed, places, shifted)]].set(jnp.asarray(sizes, jnp.int32))

    sizes = jnp.where(number % 4 == 0, named(heavy_load, number // 4), named(usual, number - number // 4 - 1))
    mixed = jax.random.permutation(jax.random.fold_in(own, 3), amount)
    giver, sink = mixed[0:amount // 2 * 2:2], mixed[1:amount // 2 * 2:2]
    slack = jnp.minimum(sizes[giver] - 1, reach - sizes[sink]) // 2
    slack = jnp.where((giver == sequence[0]) | (sink == sequence[0]) | (sizes[sink] == 0), 0, jnp.maximum(slack, 0))
    shifted = jax.random.randint(jax.random.fold_in(own, 4), (amount // 2,), 0, 1 << 20) % (slack + 1)
    sizes = sizes.at[giver].add(-shifted).at[sink].add(shifted)
    labels = jnp.searchsorted(jnp.cumsum(sizes), jnp.arange(rows * top), side="right").astype(jnp.int32)
    table = labels.reshape(top, rows).T
    table = table[jax.random.permutation(jax.random.fold_in(own, 1), rows)]
    rotation = jax.random.randint(jax.random.fold_in(own, 2), (rows, 1), 0, top)
    return jnp.take_along_axis(table, (jnp.arange(top)[None, :] + rotation) % top, axis=1)


def portions_of(number_of, total, limit, lean, full):
    loads = [(1 << 20) // math.isqrt(standing ** lean) + 1 for standing in range(1, number_of + 1)]
    largest = limit if full else min(limit, max(-(-total // number_of), total * loads[0] // sum(loads)))
    least = 1 if total - largest >= number_of - 1 else 0
    holding, surplus = [largest] + [least] * (number_of - 1), total - largest - least * (number_of - 1)
    while surplus > 0:
        candidates = [i for i in range(1, number_of) if holding[i] < largest] or [i for i in range(1, number_of) if holding[i] < limit]
        mass, budget = sum([loads[i] for i in candidates]), surplus
        for i in candidates:
            addition = min(limit - holding[i], max(1, budget * loads[i] // mass), surplus)
            holding[i] = holding[i] + addition
            surplus = surplus - addition
    return np.array(holding)


def bell_draw(own_key, shape, deviation, limit, cuts=(), kind=jnp.bfloat16):
    array = deviation * jax.random.normal(own_key, shape, jnp.float32)
    if cuts:
        array = array * block_levels(own_key, shape, cuts, -0.22, 0.18)
    return jnp.clip(array, -limit, limit).astype(kind)


def setup_inputs(seed: int = 0) -> dict:
    keys = jax.random.split(jax.random.key(seed), 14)
    hidden = bell_draw(keys[0], (SEQS, WINDOW, D), 1.0, 6.0, ((0, 8), (1, 4)))
    queries = draw_queries(jax.random.fold_in(keys[13], 71), 0)
    new_keys = bell_draw(keys[2], (SEQS, WINDOW, KVH * HD), 1.0, 6.0, ((0, 8), (1, 4)))
    new_values = bell_draw(keys[3], (SEQS, WINDOW, KVH * HD), 1.0, 6.0, ((0, 8), (1, 4)))
    cache_keys = draw_cache_keys(jax.random.fold_in(keys[13], 71), 0)
    cache_values = bell_draw(keys[5], (SEQS, CACHE, KVH * HD), 1.0, 6.0, ((0, 8), (1, 4)))
    out_weight = bell_draw(keys[6], (HQ * HD, D), 0.25, 1.5, ((0, 32),))
    norm_gain = jnp.clip(1.0 + 0.18 * jax.random.normal(keys[7], (D,), jnp.float32), 0.099609375, 1.8984375).astype(jnp.bfloat16)
    gate_proj = bell_draw(keys[8], (EXPERTS, D, MOE_FF), D ** -0.5, 0.09375, ((0, 32),))
    up_proj = bell_draw(keys[9], (EXPERTS, D, MOE_FF), D ** -0.5, 0.09375, ((0, 32),))
    down_proj = bell_draw(keys[10], (EXPERTS, MOE_FF, D), MOE_FF ** -0.5, 0.21875, ((0, 32),))
    expert_ids_keys = jax.random.split(jax.random.fold_in(keys[11], 1), SEQS * WINDOW // TOK_DEV)
    expert_ids_turns = jax.random.permutation(jax.random.fold_in(keys[11], 3), SEQS * WINDOW // TOK_DEV)
    expert_ids = jax.vmap(lambda own, number: routed_block(jax.random.fold_in(keys[11], 2), own, number, TOK_DEV, EXPERTS, TOPK, CAP, 2))(expert_ids_keys, expert_ids_turns).reshape((SEQS, WINDOW, TOPK))
    gate_fixed = set_ends(jax.random.randint(keys[12], (SEQS, WINDOW, TOPK), 1, 65536), jax.random.fold_in(keys[12], 1), 1, 65535).astype(jnp.int32)
    return {"hidden": hidden, "queries": queries, "new_keys": new_keys, "new_values": new_values, "cache_keys": cache_keys, "cache_values": cache_values, "out_weight": out_weight, "norm_gain": norm_gain, "gate_proj": gate_proj, "up_proj": up_proj, "down_proj": down_proj, "expert_ids": expert_ids, "gate_fixed": gate_fixed}


def attend_sequence(operands):
    query_rows, cached_keys, cached_values, window_keys, window_values = operands
    window = query_rows.shape[0]
    group_size = HQ // KVH
    query_heads = query_rows.reshape(window, HQ, HD).astype(jnp.float32)
    all_keys = jnp.concatenate([cached_keys, window_keys], axis=0).reshape(-1, KVH, HD).astype(jnp.float32)
    all_values = jnp.concatenate([cached_values, window_values], axis=0).reshape(-1, KVH, HD).astype(jnp.float32)
    key_heads = jnp.repeat(all_keys, group_size, axis=1)
    value_heads = jnp.repeat(all_values, group_size, axis=1)
    scores = jnp.einsum('whd,lhd->hwl', query_heads, key_heads) / math.sqrt(HD)
    positions = jnp.arange(key_heads.shape[0])[None, None, :]
    query_pos = CACHE + jnp.arange(window)[None, :, None]
    scores = jnp.where(positions <= query_pos, scores, -jnp.inf)
    highest = lax.optimization_barrier(jnp.max(scores, axis=-1, keepdims=True))
    powers = jnp.exp(scores - highest)
    weights = (powers / lax.optimization_barrier(jnp.sum(powers, axis=-1, keepdims=True))).astype(jnp.bfloat16)
    attended = jnp.einsum('hwl,lhd->whd', weights.astype(jnp.float32), value_heads)
    return attended.astype(jnp.bfloat16).reshape(window, HQ * HD)

def reference(hidden, queries, new_keys, new_values, cache_keys, cache_values, out_weight, norm_gain, gate_proj, up_proj, down_proj, expert_ids, gate_fixed):
    attended = lax.map(attend_sequence, (queries, cache_keys, cache_values, new_keys, new_values))
    rows_all = SEQS * WINDOW
    flat_att = attended.reshape(rows_all, HQ * HD)
    group_width = HQ * HD // N_CTX
    summed = jnp.zeros((rows_all, D), jnp.float32)
    for member in range(N_CTX):
        partial_sum = jnp.dot(flat_att[:, member * group_width:(member + 1) * group_width], out_weight[member * group_width:(member + 1) * group_width], preferred_element_type=jnp.float32).astype(jnp.bfloat16)
        partial_sum = lax.optimization_barrier(partial_sum)
        summed = summed + partial_sum.astype(jnp.float32)
    after_attention = (hidden.reshape(rows_all, D).astype(jnp.float32) + summed).astype(jnp.bfloat16)
    after_float = after_attention.astype(jnp.float32)
    normed = (after_float * lax.rsqrt(lax.optimization_barrier(jnp.mean(after_float * after_float, axis=-1, keepdims=True)) + 1e-06) * norm_gain.astype(jnp.float32)).astype(jnp.bfloat16)
    flat_ids = expert_ids.reshape(-1).astype(jnp.int32)
    sorted_order = jnp.argsort(flat_ids, stable=True).astype(jnp.int32)
    counts = lax.optimization_barrier(jnp.sum((flat_ids[:, None] == jnp.arange(EXPERTS, dtype=jnp.int32)[None, :]).astype(jnp.int32), axis=0)).astype(jnp.int32)
    offsets = (jnp.cumsum(counts) - counts).astype(jnp.int32)
    slot_total = CAP * N_CTX * N_EXP
    padded = jnp.concatenate([sorted_order, jnp.zeros((slot_total,), jnp.int32)])
    gate_share = gate_fixed.reshape(-1).astype(jnp.float32) / 65536.0

    def one_expert(accumulated, operands):
        weight_gate, weight_up, weight_down, offset, number = operands
        chosen = lax.dynamic_slice_in_dim(padded, offset.astype(jnp.int32), slot_total)
        live_slots = jnp.arange(slot_total, dtype=jnp.int32) < number
        token_rows = (chosen // TOPK).astype(jnp.int32)
        scaled = jnp.where(live_slots, gate_share[chosen], jnp.zeros((slot_total,), jnp.float32))
        inputs = normed[token_rows]
        gate_act = jnp.dot(inputs, weight_gate, preferred_element_type=jnp.float32)
        up_act = jnp.dot(inputs, weight_up, preferred_element_type=jnp.float32)
        product = (jax.nn.silu(gate_act) * up_act).astype(jnp.bfloat16)
        output = jnp.dot(product, weight_down, preferred_element_type=jnp.float32).astype(jnp.bfloat16)
        accumulated = accumulated.at[token_rows].add(scaled[:, None] * output.astype(jnp.float32))
        return (accumulated, None)
    expert_sum, _ = lax.scan(one_expert, jnp.zeros((rows_all, D), jnp.float32), (gate_proj, up_proj, down_proj, offsets, counts))
    layer_output = (after_float + expert_sum).astype(jnp.bfloat16)
    return (after_attention.reshape(SEQS, WINDOW, D), layer_output.reshape(SEQS, WINDOW, D))
```

```python
import functools
import math

import jax
import jax.numpy as jnp
from jax import lax
from jax.experimental import pallas as pl
from jax.experimental.pallas import tpu as pltpu
from jax.sharding import Mesh
from jax.sharding import PartitionSpec as P

D = 4096
KVH = 4
HD = 128
TOPK = 4
AXES = ("y", "c", "z", "x")
PLANE = ("y", "c", "x")
BF = jnp.bfloat16
F32 = jnp.float32


def widen_heads(tensor, copies):
    row_count = tensor.shape[0]
    heads = tensor.reshape(row_count, KVH, HD)
    return jnp.repeat(heads, copies, axis=1).reshape(row_count, KVH * copies * HD)


def expert_ffn(incoming, gate_matrix, up_matrix, down_matrix):
    shape_in = incoming.shape
    flat_rows = incoming.reshape(-1, shape_in[-1])
    gate_act = jnp.dot(flat_rows, gate_matrix, preferred_element_type=jnp.float32)
    up_act = jnp.dot(flat_rows, up_matrix, preferred_element_type=jnp.float32)
    product = (jax.nn.silu(gate_act) * up_act).astype(jnp.bfloat16)
    output = jnp.dot(product, down_matrix, preferred_element_type=jnp.float32)
    return output.astype(jnp.bfloat16).reshape(shape_in)


def general_device(
    hidden,
    queries,
    new_keys,
    new_values,
    cache_keys,
    cache_values,
    out_weight,
    norm_gain,
    gate_proj,
    up_proj,
    down_proj,
    expert_ids,
    gate_fixed,
):
    context = lax.axis_size("ctx")
    experts_all = context * lax.axis_size("exp")
    tok_rows = hidden.shape[1]
    copies = context // KVH
    local_queries = queries[0]
    query_part, key_new, value_new, key_old, value_old = (
        lax.all_to_all(local_queries, "ctx", split_axis=1, concat_axis=0, tiled=True),
        lax.all_to_all(
            widen_heads(new_keys[0], copies), "ctx", split_axis=1, concat_axis=0, tiled=True
        ),
        lax.all_to_all(
            widen_heads(new_values[0], copies), "ctx", split_axis=1, concat_axis=0, tiled=True
        ),
        lax.all_to_all(
            widen_heads(cache_keys[0], copies), "ctx", split_axis=1, concat_axis=0, tiled=True
        ),
        lax.all_to_all(
            widen_heads(cache_values[0], copies), "ctx", split_axis=1, concat_axis=0, tiled=True
        ),
    )
    key_rows = jnp.concatenate([key_old, key_new], axis=0)
    value_rows = jnp.concatenate([value_old, value_new], axis=0)
    window = query_part.shape[0]
    heads_here = query_part.shape[1] // HD
    total_cache = key_old.shape[0]
    block_rows = min(512, window)
    block_count = window // block_rows
    key_pos = jnp.arange(key_rows.shape[0])

    def attend(operands):
        query_block, block_start = operands
        query_heads = query_block.reshape(block_rows, heads_here, HD)
        scores = jnp.einsum(
            "whd,ld->hwl", query_heads, key_rows, preferred_element_type=jnp.float32
        ) / math.sqrt(HD)
        query_pos = total_cache + block_start + jnp.arange(block_rows)
        scores = jnp.where(key_pos[None, None, :] <= query_pos[None, :, None], scores, -jnp.inf)
        highest = jnp.max(scores, axis=-1, keepdims=True)
        powers = jnp.exp(scores - highest)
        weights = (powers / jnp.sum(powers, axis=-1, keepdims=True)).astype(jnp.bfloat16)
        attended_block = jnp.einsum(
            "hwl,ld->whd", weights, value_rows, preferred_element_type=jnp.float32
        )
        return attended_block.astype(jnp.bfloat16).reshape(block_rows, heads_here * HD)

    attended = lax.map(
        attend,
        (
            query_part.reshape(block_count, block_rows, heads_here * HD),
            jnp.arange(block_count) * block_rows,
        ),
    ).reshape(window, heads_here * HD)
    proj_rows = lax.all_gather(out_weight, "exp", axis=0, tiled=True)
    projected = lax.psum_scatter(
        jnp.dot(attended, proj_rows, preferred_element_type=jnp.float32).astype(jnp.bfloat16),
        "ctx",
        scatter_dimension=0,
        tiled=True,
    ).astype(jnp.float32)
    after_attention = (hidden[0].astype(jnp.float32) + projected).astype(jnp.bfloat16)
    after_float = after_attention.astype(jnp.float32)
    normed = (
        after_float
        * lax.rsqrt(jnp.mean(after_float * after_float, axis=-1, keepdims=True) + 1e-06)
        * norm_gain.astype(jnp.float32)
    ).astype(jnp.bfloat16)
    capacity = max(2, 2 * tok_rows * TOPK // experts_all)
    flat_ids = expert_ids[0].reshape(-1)
    one_hot = (flat_ids[:, None] == jnp.arange(experts_all, dtype=jnp.int32)[None, :]).astype(
        jnp.int32
    )
    earlier = jnp.cumsum(one_hot, axis=0) - one_hot
    slot_index = jnp.sum(earlier * one_hot, axis=1)
    target = flat_ids * capacity + slot_index
    sources = jnp.repeat(normed, TOPK, axis=0)
    outgoing = jnp.zeros((experts_all * capacity, D), jnp.bfloat16).at[target].set(sources)
    results = expert_ffn(
        lax.all_to_all(
            outgoing.reshape(experts_all, capacity, D),
            ("ctx", "exp"),
            split_axis=0,
            concat_axis=0,
            tiled=True,
        ),
        gate_proj[0],
        up_proj[0],
        down_proj[0],
    )
    returned = lax.all_to_all(results, ("ctx", "exp"), split_axis=0, concat_axis=0, tiled=True)
    back_rows = returned.reshape(experts_all * capacity, D)[target]
    shares = gate_fixed[0].astype(jnp.float32) / 65536.0
    expert_sum = jnp.sum(
        back_rows.astype(jnp.float32).reshape(tok_rows, TOPK, D) * shares[:, :, None], axis=1
    )
    layer_output = (after_float + expert_sum).astype(jnp.bfloat16)
    return (after_attention[None], layer_output[None])


def pairs_of(sizes, axis, target):
    found = []
    for i in range(sizes[axis]):
        j = target(i)
        if j is not None:
            found.append((i, j))
    return found


def swap(value, axis):
    return lax.ppermute(value, axis, [(0, 1), (1, 0)])


def upward(value, first, last):
    return lax.ppermute(value, "z", [(z, z + 1) for z in range(first, last + 1)])


def downward(value, first, last):
    return lax.ppermute(value, "z", [(z, z - 1) for z in range(first, last + 1)])


def pick(z, options):
    result = options[3]
    for index in (2, 1, 0):
        result = jnp.where(z == index, options[index], result)
    return result


def along_z(own, z):
    up1, down1 = upward(own, 0, 2), downward(own, 1, 3)
    up2, down2 = upward(up1, 1, 2), downward(down1, 1, 2)
    up3, down3 = upward(up2, 2, 2), downward(down2, 1, 1)
    return [
        own,
        pick(z, (down1, up1, down1, up1)),
        pick(z, (down2, down1, up1, up2)),
        pick(z, (down3, down2, up2, up3)),
    ]


SOURCES = ((0, 1, 2, 3), (1, 0, 2, 3), (2, 3, 1, 0), (3, 2, 1, 0))


def attend_kernel(message_ref, out_ref, keys, values, *, group, tokens):
    width = group * HD
    blocks = message_ref.shape[0]
    cached = blocks * tokens
    for s in range(blocks):
        rows = pl.ds(s * tokens, tokens)
        later = pl.ds(cached + s * tokens, tokens)
        keys[rows, :] = message_ref[s, :, width : width + HD]
        keys[later, :] = message_ref[s, :, width + HD : width + 2 * HD]
        values[rows, :] = message_ref[s, :, width + 2 * HD : width + 3 * HD]
        values[later, :] = message_ref[s, :, width + 3 * HD : width + 4 * HD]
    factor = math.log2(math.e) / math.sqrt(HD)
    row = lax.broadcasted_iota(jnp.int32, (tokens, tokens), 0)
    column = lax.broadcasted_iota(jnp.int32, (tokens, tokens), 1)
    allowed = jnp.concatenate([column <= row] * 2, axis=0)
    for s in range(blocks):
        before = cached + s * tokens

        def two_heads(step, carry):
            first = pl.multiple_of(step * 2 * HD, 2 * HD)
            second = pl.multiple_of(step * 2 * HD + HD, HD)
            queries = jnp.concatenate(
                [message_ref[s, :, pl.ds(first, HD)], message_ref[s, :, pl.ds(second, HD)]], axis=0
            )
            dims = (((1,), (1,)), ((), ()))
            old = lax.dot_general(
                queries, keys[:before, :], dims, preferred_element_type=F32
            )
            own = lax.dot_general(
                queries, keys[before : before + tokens, :], dims, preferred_element_type=F32
            )
            own = jnp.where(allowed, own, -jnp.inf)
            highest = jnp.maximum(
                jnp.max(old, axis=-1, keepdims=True), jnp.max(own, axis=-1, keepdims=True)
            )
            old = jnp.exp2((old - highest) * factor)
            own = jnp.exp2((own - highest) * factor)
            total = jnp.sum(old, axis=-1, keepdims=True) + jnp.sum(own, axis=-1, keepdims=True)
            mixed = jnp.dot(old.astype(BF), values[:before, :], preferred_element_type=F32)
            mixed += jnp.dot(
                own.astype(BF), values[before : before + tokens, :], preferred_element_type=F32
            )
            mixed = (mixed / total).astype(BF)
            out_ref[pl.ds(s * tokens, tokens), pl.ds(first, HD)] = mixed[:tokens]
            out_ref[pl.ds(s * tokens, tokens), pl.ds(second, HD)] = mixed[tokens:]
            return carry

        lax.fori_loop(0, group // 2, two_heads, 0)


def attention(message, group):
    blocks, tokens, _ = message.shape
    window = blocks * tokens
    live = blocks * tokens + tokens * (blocks + 1) // 2
    return pl.pallas_call(
        functools.partial(attend_kernel, group=group, tokens=tokens),
        out_shape=jax.ShapeDtypeStruct((window, group * HD), BF),
        in_specs=[pl.BlockSpec(memory_space=pltpu.VMEM)],
        out_specs=pl.BlockSpec(memory_space=pltpu.VMEM),
        scratch_shapes=[pltpu.VMEM((2 * window, HD), BF), pltpu.VMEM((2 * window, HD), BF)],
        compiler_params=pltpu.CompilerParams(vmem_limit_bytes=32 * 2**20),
        cost_estimate=pl.CostEstimate(
            flops=4 * window * group * HD * live,
            bytes_accessed=2 * message.size + 2 * window * group * HD,
            transcendentals=window * group * live,
        ),
        name="attention",
    )(message)


def routing(ids, gates, z):
    tokens = ids.shape[0]
    plane = 8
    both = along_z(jnp.concatenate([ids, gates], axis=1), z)
    both = jnp.stack(both)
    ids4, gates4 = both[..., :TOPK], both[..., TOPK:]
    place = jnp.arange(plane)
    y, c, x = place // 4, place // 2 % 2, place % 2
    experts = (y * 2 + c) * 8 + z * 2 + x
    capacity = max(2, 2 * tokens * TOPK // 32)
    same = ids4[:, None] == experts[None, :, None, None]
    chosen = same.any(-1)
    gate = jnp.sum(jnp.where(same, gates4[:, None], 0), axis=-1)
    earlier = (jnp.arange(tokens)[:, None] < jnp.arange(tokens)[None, :]).astype(BF)
    rank = jnp.dot(
        chosen.astype(BF).reshape(4 * plane, tokens), earlier, preferred_element_type=F32
    )
    rank = rank.reshape(4, plane, 1, tokens).astype(jnp.int32)
    at_slot = chosen[:, :, None, :] & (rank == jnp.arange(capacity)[None, None, :, None])
    high = (gate >> 8).astype(F32) / 256.0
    low = (gate & 255).astype(F32) / 65536.0
    slots = plane * capacity

    def spread(part):
        return jnp.where(at_slot, part[:, :, None, :], 0.0).astype(BF).reshape(4, slots, tokens)

    places = at_slot.astype(BF).reshape(4, slots, tokens)
    shares = jnp.concatenate([spread(high), spread(low)], axis=-1)
    return places, shares


def plane_exchange(rows):
    blocks = rows.reshape(8, -1, D)
    return lax.all_to_all(blocks, PLANE, split_axis=0, concat_axis=0, tiled=True).reshape(-1, D)


def tuned_device(
    hidden,
    queries,
    new_keys,
    new_values,
    cache_keys,
    cache_values,
    out_weight,
    norm_gain,
    gate_proj,
    up_proj,
    down_proj,
    expert_ids,
    gate_fixed,
):
    y, c, z, x = (lax.axis_index(axis) for axis in AXES)
    tokens = hidden.shape[1]
    group = queries.shape[2] // HD // KVH
    source = jnp.array(SOURCES, jnp.int32)[z]

    def by_head(value):
        return value[0].reshape(tokens, KVH, -1).transpose(1, 0, 2)

    message = jnp.concatenate(
        [by_head(v) for v in (queries, cache_keys, new_keys, cache_values, new_values)], axis=-1
    )
    message = lax.all_to_all(message, ("y", "c"), split_axis=0, concat_axis=0, tiled=True)
    attended = attention(message, group)

    heads = [source[k] * 2 + x for k in range(4)] + [source[k] * 2 + (1 - x) for k in range(4)]
    in_order = jnp.concatenate(
        [lax.dynamic_slice_in_dim(attended, h * HD, HD, axis=1) for h in heads], axis=1
    )
    parts = 2
    width = D // parts
    projected = []
    for part in range(parts):
        mine = out_weight[:, part * width : (part + 1) * width]
        line = along_z(mine, z)
        weight = jnp.concatenate(line + [swap(block, "x") for block in line], axis=0)
        partial = jnp.dot(in_order, weight, preferred_element_type=F32)
        partial = partial.reshape(2, 2, tokens, width)
        other = lax.dynamic_index_in_dim(partial, 1 - c, 1, keepdims=False).astype(BF)
        both = lax.dynamic_index_in_dim(partial, c, 1, keepdims=False) + swap(other, "c").astype(F32)
        other = lax.dynamic_index_in_dim(both, 1 - y, 0, keepdims=False).astype(BF)
        own = lax.dynamic_index_in_dim(both, y, 0, keepdims=False)
        projected.append(own + swap(other, "y").astype(F32))
    after_attention = (
        hidden[0].astype(F32) + jnp.concatenate(projected, axis=1)
    ).astype(BF)
    after_float = after_attention.astype(F32)
    normed = (
        after_float
        * lax.rsqrt(jnp.mean(after_float * after_float, axis=-1, keepdims=True) + 1e-06)
        * norm_gain.astype(F32)
    ).astype(BF)

    places, shares = routing(expert_ids[0], gate_fixed[0], z)
    blocks = along_z(normed, z)
    results = []
    for k in range(4):
        sent = jnp.dot(places[k], blocks[k], preferred_element_type=F32).astype(BF)
        results.append(expert_ffn(plane_exchange(sent), gate_proj[0], up_proj[0], down_proj[0]))
    sums = [None] * 4
    for k in (3, 2, 1, 0):
        returned = plane_exchange(results[k])
        both = lax.dot_general(
            shares[k], returned, (((0,), (0,)), ((), ())), preferred_element_type=F32
        )
        sums[k] = both[:tokens] + both[tokens:]
    own, near, middle, far = sums

    up = upward(far.astype(BF), 0, 0)
    down = downward(far.astype(BF), 3, 3)
    up = upward((jnp.where(z == 0, middle, far) + up.astype(F32)).astype(BF), 0, 1)
    down = downward((jnp.where(z == 3, middle, far) + down.astype(F32)).astype(BF), 2, 3)
    up = upward((jnp.where(z == 1, middle, near) + up.astype(F32)).astype(BF), 0, 2)
    down = downward((jnp.where(z == 2, middle, near) + down.astype(F32)).astype(BF), 1, 3)
    layer_output = (after_float + own + up.astype(F32) + down.astype(F32)).astype(BF)
    return (after_attention[None], layer_output[None])


def solution(mesh):
    sizes = (mesh.shape["ctx"], mesh.shape["exp"])
    if sizes == (4, 8):
        inner = Mesh(mesh.devices.reshape(2, 2, 4, 2), AXES)
        ctx, exp = ("y", "c"), ("z", "x")
        body = tuned_device
    else:
        inner, ctx, exp, body = mesh, "ctx", "exp", general_device
    both = (*AXES,) if body is tuned_device else ("ctx", "exp")
    token = P(exp, ctx, None)
    expert = P(both, None, None)
    return jax.shard_map(
        body,
        mesh=inner,
        in_specs=(
            token,
            token,
            token,
            token,
            token,
            token,
            P(both, None),
            P(),
            expert,
            expert,
            expert,
            token,
            token,
        ),
        out_specs=(token, token),
        check_vma=False,
    )
```

```python
import functools
import math

import jax
import jax.numpy as jnp
from jax import lax
from jax.experimental import pallas as pl
from jax.experimental.pallas import tpu as pltpu
from jax.sharding import Mesh
from jax.sharding import PartitionSpec as P

D = 4096
KVH = 4
HD = 128
TOPK = 4
AXES = ("y", "c", "z", "x")
PLANE = ("y", "c", "x")
BF = jnp.bfloat16
VMEM = 20 * 2**20
F32 = jnp.float32


def widen_heads(tensor, copies):
    row_count = tensor.shape[0]
    heads = tensor.reshape(row_count, KVH, HD)
    return jnp.repeat(heads, copies, axis=1).reshape(row_count, KVH * copies * HD)


def expert_ffn(incoming, gate_matrix, up_matrix, down_matrix):
    shape_in = incoming.shape
    flat_rows = incoming.reshape(-1, shape_in[-1])
    gate_act = jnp.dot(flat_rows, gate_matrix, preferred_element_type=jnp.float32)
    up_act = jnp.dot(flat_rows, up_matrix, preferred_element_type=jnp.float32)
    product = (jax.nn.silu(gate_act) * up_act).astype(jnp.bfloat16)
    output = jnp.dot(product, down_matrix, preferred_element_type=jnp.float32)
    return output.astype(jnp.bfloat16).reshape(shape_in)


def general_device(
    hidden,
    queries,
    new_keys,
    new_values,
    cache_keys,
    cache_values,
    out_weight,
    norm_gain,
    gate_proj,
    up_proj,
    down_proj,
    expert_ids,
    gate_fixed,
):
    context = lax.axis_size("ctx")
    experts_all = context * lax.axis_size("exp")
    tok_rows = hidden.shape[1]
    copies = context // KVH
    local_queries = queries[0]
    query_part, key_new, value_new, key_old, value_old = (
        lax.all_to_all(local_queries, "ctx", split_axis=1, concat_axis=0, tiled=True),
        lax.all_to_all(
            widen_heads(new_keys[0], copies), "ctx", split_axis=1, concat_axis=0, tiled=True
        ),
        lax.all_to_all(
            widen_heads(new_values[0], copies), "ctx", split_axis=1, concat_axis=0, tiled=True
        ),
        lax.all_to_all(
            widen_heads(cache_keys[0], copies), "ctx", split_axis=1, concat_axis=0, tiled=True
        ),
        lax.all_to_all(
            widen_heads(cache_values[0], copies), "ctx", split_axis=1, concat_axis=0, tiled=True
        ),
    )
    key_rows = jnp.concatenate([key_old, key_new], axis=0)
    value_rows = jnp.concatenate([value_old, value_new], axis=0)
    window = query_part.shape[0]
    heads_here = query_part.shape[1] // HD
    total_cache = key_old.shape[0]
    block_rows = min(512, window)
    block_count = window // block_rows
    key_pos = jnp.arange(key_rows.shape[0])

    def attend(operands):
        query_block, block_start = operands
        query_heads = query_block.reshape(block_rows, heads_here, HD)
        scores = jnp.einsum(
            "whd,ld->hwl", query_heads, key_rows, preferred_element_type=jnp.float32
        ) / math.sqrt(HD)
        query_pos = total_cache + block_start + jnp.arange(block_rows)
        scores = jnp.where(key_pos[None, None, :] <= query_pos[None, :, None], scores, -jnp.inf)
        highest = jnp.max(scores, axis=-1, keepdims=True)
        powers = jnp.exp(scores - highest)
        weights = (powers / jnp.sum(powers, axis=-1, keepdims=True)).astype(jnp.bfloat16)
        attended_block = jnp.einsum(
            "hwl,ld->whd", weights, value_rows, preferred_element_type=jnp.float32
        )
        return attended_block.astype(jnp.bfloat16).reshape(block_rows, heads_here * HD)

    attended = lax.map(
        attend,
        (
            query_part.reshape(block_count, block_rows, heads_here * HD),
            jnp.arange(block_count) * block_rows,
        ),
    ).reshape(window, heads_here * HD)
    proj_rows = lax.all_gather(out_weight, "exp", axis=0, tiled=True)
    projected = lax.psum_scatter(
        jnp.dot(attended, proj_rows, preferred_element_type=jnp.float32).astype(jnp.bfloat16),
        "ctx",
        scatter_dimension=0,
        tiled=True,
    ).astype(jnp.float32)
    after_attention = (hidden[0].astype(jnp.float32) + projected).astype(jnp.bfloat16)
    after_float = after_attention.astype(jnp.float32)
    normed = (
        after_float
        * lax.rsqrt(jnp.mean(after_float * after_float, axis=-1, keepdims=True) + 1e-06)
        * norm_gain.astype(jnp.float32)
    ).astype(jnp.bfloat16)
    capacity = max(2, 2 * tok_rows * TOPK // experts_all)
    flat_ids = expert_ids[0].reshape(-1)
    one_hot = (flat_ids[:, None] == jnp.arange(experts_all, dtype=jnp.int32)[None, :]).astype(
        jnp.int32
    )
    earlier = jnp.cumsum(one_hot, axis=0) - one_hot
    slot_index = jnp.sum(earlier * one_hot, axis=1)
    target = flat_ids * capacity + slot_index
    sources = jnp.repeat(normed, TOPK, axis=0)
    outgoing = jnp.zeros((experts_all * capacity, D), jnp.bfloat16).at[target].set(sources)
    results = expert_ffn(
        lax.all_to_all(
            outgoing.reshape(experts_all, capacity, D),
            ("ctx", "exp"),
            split_axis=0,
            concat_axis=0,
            tiled=True,
        ),
        gate_proj[0],
        up_proj[0],
        down_proj[0],
    )
    returned = lax.all_to_all(results, ("ctx", "exp"), split_axis=0, concat_axis=0, tiled=True)
    back_rows = returned.reshape(experts_all * capacity, D)[target]
    shares = gate_fixed[0].astype(jnp.float32) / 65536.0
    expert_sum = jnp.sum(
        back_rows.astype(jnp.float32).reshape(tok_rows, TOPK, D) * shares[:, :, None], axis=1
    )
    layer_output = (after_float + expert_sum).astype(jnp.bfloat16)
    return (after_attention[None], layer_output[None])


def swap(value, axis):
    return lax.ppermute(value, axis, [(0, 1), (1, 0)])


def along(value, pairs):
    return lax.ppermute(value, "z", pairs)


OUTER = [(0, 1), (1, 0), (2, 3), (3, 2)]
INNER = [(1, 2), (2, 1)]
OUTWARD = [(1, 0), (2, 3)]
INWARD = [(0, 1), (3, 2)]

SOURCES = ((0, 1, 2, 3), (1, 0, 2, 3), (2, 3, 1, 0), (3, 2, 1, 0))


def along_z(own, inner):
    near, middle_in = along(own, OUTER), along(own, INNER)
    middle_out, far_in = along(middle_in, OUTWARD), along(near, INNER)
    far_out = along(far_in, OUTWARD)
    return [own, near, jnp.where(inner, middle_in, middle_out), jnp.where(inner, far_in, far_out)]


def attend_kernel(message_ref, out_ref, keys, values, *, group, tokens):
    width = group * HD
    blocks = message_ref.shape[0]
    cached = blocks * tokens
    for s in range(blocks):
        rows = pl.ds(s * tokens, tokens)
        later = pl.ds(cached + s * tokens, tokens)
        keys[rows, :] = message_ref[s, :, width : width + HD]
        keys[later, :] = message_ref[s, :, width + HD : width + 2 * HD]
        values[rows, :] = message_ref[s, :, width + 2 * HD : width + 3 * HD]
        values[later, :] = message_ref[s, :, width + 3 * HD : width + 4 * HD]
    factor = math.log2(math.e) / math.sqrt(HD)
    row = lax.broadcasted_iota(jnp.int32, (tokens, tokens), 0)
    column = lax.broadcasted_iota(jnp.int32, (tokens, tokens), 1)
    allowed = jnp.concatenate([column <= row] * 2, axis=0)
    for s in range(blocks):
        before = cached + s * tokens

        def two_heads(step, carry):
            first = pl.multiple_of(step * 2 * HD, 2 * HD)
            second = pl.multiple_of(step * 2 * HD + HD, HD)
            queries = jnp.concatenate(
                [message_ref[s, :, pl.ds(first, HD)], message_ref[s, :, pl.ds(second, HD)]], axis=0
            )
            dims = (((1,), (1,)), ((), ()))
            old = lax.dot_general(
                queries, keys[:before, :], dims, preferred_element_type=F32
            )
            own = lax.dot_general(
                queries, keys[before : before + tokens, :], dims, preferred_element_type=F32
            )
            own = jnp.where(allowed, own, -jnp.inf)
            highest = jnp.maximum(
                jnp.max(old, axis=-1, keepdims=True), jnp.max(own, axis=-1, keepdims=True)
            )
            old = jnp.exp2((old - highest) * factor)
            own = jnp.exp2((own - highest) * factor)
            total = jnp.sum(old, axis=-1, keepdims=True) + jnp.sum(own, axis=-1, keepdims=True)
            mixed = jnp.dot(old.astype(BF), values[:before, :], preferred_element_type=F32)
            mixed += jnp.dot(
                own.astype(BF), values[before : before + tokens, :], preferred_element_type=F32
            )
            mixed = (mixed / total).astype(BF)
            out_ref[pl.ds(s * tokens, tokens), pl.ds(first, HD)] = mixed[:tokens]
            out_ref[pl.ds(s * tokens, tokens), pl.ds(second, HD)] = mixed[tokens:]
            return carry

        lax.fori_loop(0, group // 2, two_heads, 0)


def attention(message, group):
    blocks, tokens, _ = message.shape
    window = blocks * tokens
    live = blocks * tokens + tokens * (blocks + 1) // 2
    return pl.pallas_call(
        functools.partial(attend_kernel, group=group, tokens=tokens),
        out_shape=jax.ShapeDtypeStruct((window, group * HD), BF),
        in_specs=[pl.BlockSpec(memory_space=pltpu.VMEM)],
        out_specs=pl.BlockSpec(memory_space=pltpu.VMEM),
        scratch_shapes=[pltpu.VMEM((2 * window, HD), BF), pltpu.VMEM((2 * window, HD), BF)],
        compiler_params=pltpu.CompilerParams(vmem_limit_bytes=32 * 2**20),
        cost_estimate=pl.CostEstimate(
            flops=4 * window * group * HD * live,
            bytes_accessed=2 * message.size + 2 * window * group * HD,
            transcendentals=window * group * live,
        ),
        name="attention",
    )(message)


def routing(ids, gates, z, inner):
    tokens = ids.shape[0]
    plane = 8
    both = along_z(jnp.concatenate([ids, gates], axis=1), inner)
    both = jnp.stack(both)
    ids4, gates4 = both[..., :TOPK], both[..., TOPK:]
    place = jnp.arange(plane)
    y, c, x = place // 4, place // 2 % 2, place % 2
    experts = (y * 2 + c) * 8 + z * 2 + x
    capacity = max(2, 2 * tokens * TOPK // 32)
    same = ids4[:, None] == experts[None, :, None, None]
    chosen = same.any(-1)
    gate = jnp.sum(jnp.where(same, gates4[:, None], 0), axis=-1)
    earlier = (jnp.arange(tokens)[:, None] < jnp.arange(tokens)[None, :]).astype(BF)
    rank = jnp.dot(
        chosen.astype(BF).reshape(4 * plane, tokens), earlier, preferred_element_type=F32
    )
    rank = rank.reshape(4, plane, 1, tokens).astype(jnp.int32)
    at_slot = chosen[:, :, None, :] & (rank == jnp.arange(capacity)[None, None, :, None])
    high = (gate >> 8).astype(F32) / 256.0
    low = (gate & 255).astype(F32) / 65536.0
    slots = plane * capacity

    def spread(part):
        return jnp.where(at_slot, part[:, :, None, :], 0.0).astype(BF).reshape(4, slots, tokens)

    places = at_slot.astype(BF).reshape(4, slots, tokens)
    shares = jnp.concatenate([spread(high), spread(low)], axis=-1).transpose(0, 2, 1)
    return places, shares


def plane_exchange(rows):
    blocks = rows.reshape(8, -1, D)
    return lax.all_to_all(blocks, PLANE, split_axis=0, concat_axis=0, tiled=True).reshape(-1, D)


def experts_kernel(*refs, blocks, steps):
    rows, (gate_ref, up_ref, down_ref) = refs[:blocks], refs[blocks : blocks + 3]
    outs, (gate, up, product) = refs[blocks + 3 : 2 * blocks + 3], refs[2 * blocks + 3 :]
    step = pl.program_id(0)
    count = rows[0].shape[0]
    spans = [pl.ds(block * count, count) for block in range(blocks)]

    @pl.when(step < steps)
    def _():
        for ref, span in zip(rows, spans):
            more_gate = jnp.dot(ref[...], gate_ref[0], preferred_element_type=F32)
            more_up = jnp.dot(ref[...], up_ref[0], preferred_element_type=F32)

            @pl.when(step == 0)
            def _():
                gate[span, :] = more_gate
                up[span, :] = more_up

            @pl.when((step > 0) & (step < steps - 1))
            def _():
                gate[span, :] += more_gate
                up[span, :] += more_up

            @pl.when(step == steps - 1)
            def _():
                total = gate[span, :] + more_gate
                silu = total / (1.0 + jnp.exp(-total))
                product[span, :] = (silu * (up[span, :] + more_up)).astype(BF)

    @pl.when(step >= steps)
    def _():
        for ref, span in zip(outs, spans):
            ref[...] = jnp.dot(
                product[span, :], down_ref[0], preferred_element_type=F32
            ).astype(BF)


def experts(blocks, gate_proj, up_proj, down_proj):
    count, hidden = blocks[0].shape[0], gate_proj.shape[2]
    total = count * len(blocks)
    steps = 4
    tile = D // steps
    read = pl.BlockSpec((count, tile), lambda j: (0, jnp.minimum(j, steps - 1)))
    write = pl.BlockSpec((count, tile), lambda j: (0, jnp.maximum(j - steps, 0)))
    inner = pl.BlockSpec((1, tile, hidden), lambda j: (0, jnp.minimum(j, steps - 1), 0))
    outer = pl.BlockSpec((1, hidden, tile), lambda j: (0, 0, jnp.maximum(j - steps, 0)))
    return pl.pallas_call(
        functools.partial(experts_kernel, blocks=len(blocks), steps=steps),
        grid=(2 * steps,),
        out_shape=[jax.ShapeDtypeStruct((count, D), BF)] * len(blocks),
        in_specs=[read] * len(blocks) + [inner, inner, outer],
        out_specs=[write] * len(blocks),
        scratch_shapes=[
            pltpu.VMEM((total, hidden), F32),
            pltpu.VMEM((total, hidden), F32),
            pltpu.VMEM((total, hidden), BF),
        ],
        compiler_params=pltpu.CompilerParams(vmem_limit_bytes=30 * 2**20),
        cost_estimate=pl.CostEstimate(
            flops=total, bytes_accessed=total, transcendentals=0
        ),
        name="experts",
    )(*blocks, gate_proj, up_proj, down_proj)


def expert_kernel(rows_ref, gate_ref, up_ref, down_ref, out_ref, total):
    step = pl.program_id(0)
    rows = rows_ref[...]
    gate = jnp.dot(rows, gate_ref[0], preferred_element_type=F32)
    up = jnp.dot(rows, up_ref[0], preferred_element_type=F32)
    product = (gate / (1.0 + jnp.exp(-gate)) * up).astype(BF)
    output = jnp.dot(product, down_ref[0], preferred_element_type=F32)

    @pl.when(step == 0)
    def _():
        total[...] = output

    @pl.when((step > 0) & (step < pl.num_programs(0) - 1))
    def _():
        total[...] += output

    @pl.when(step == pl.num_programs(0) - 1)
    def _():
        out_ref[...] = (total[...] + output).astype(BF)


def expert(rows, gate_proj, up_proj, down_proj):
    count, hidden = rows.shape[0], gate_proj.shape[2]
    tile = 256
    return pl.pallas_call(
        expert_kernel,
        grid=(hidden // tile,),
        out_shape=jax.ShapeDtypeStruct(rows.shape, BF),
        in_specs=[
            pl.BlockSpec((count, D), lambda j: (0, 0)),
            pl.BlockSpec((1, D, tile), lambda j: (0, 0, j)),
            pl.BlockSpec((1, D, tile), lambda j: (0, 0, j)),
            pl.BlockSpec((1, tile, D), lambda j: (0, j, 0)),
        ],
        out_specs=pl.BlockSpec((count, D), lambda j: (0, 0)),
        scratch_shapes=[pltpu.VMEM((count, D), F32)],
        compiler_params=pltpu.CompilerParams(vmem_limit_bytes=40 * 2**20),
        cost_estimate=pl.CostEstimate(
            flops=6 * count * D * hidden,
            bytes_accessed=6 * D * hidden + 4 * count * D,
            transcendentals=count * hidden,
        ),
        name="expert",
    )(rows, gate_proj, up_proj, down_proj)


def combine_kernel(share_ref, rows_ref, *refs):
    *added, out_ref = refs
    both = jnp.dot(share_ref[...], rows_ref[...], preferred_element_type=F32)
    tokens = out_ref.shape[0]
    total = both[:tokens] + both[tokens:]
    for ref in added:
        total += ref[...].astype(F32)
    out_ref[...] = total.astype(out_ref.dtype)


def combine(share, rows, *added):
    slots = rows.shape[0]
    tokens = share.shape[0] // 2
    tile = D // 2
    block = pl.BlockSpec((tokens, tile), lambda j: (0, j))
    return pl.pallas_call(
        combine_kernel,
        grid=(D // tile,),
        out_shape=jax.ShapeDtypeStruct((tokens, D), BF),
        in_specs=[
            pl.BlockSpec((2 * tokens, slots), lambda j: (0, 0)),
            pl.BlockSpec((slots, tile), lambda j: (0, j)),
        ]
        + [block] * len(added),
        out_specs=block,
        compiler_params=pltpu.CompilerParams(vmem_limit_bytes=VMEM),
        cost_estimate=pl.CostEstimate(
            flops=tokens, bytes_accessed=tokens, transcendentals=0
        ),
        name="combine",
    )(share, rows, *added)


def slots_kernel(place_ref, *refs):
    *blocks, out_ref = refs
    block = blocks[0][...]
    for ref in blocks[1:]:
        block = block + ref[...]
    out_ref[...] = jnp.dot(place_ref[...], block, preferred_element_type=F32).astype(BF)


def slots_of(place, *blocks):
    slots, tokens = place.shape
    tile = D // 2
    return pl.pallas_call(
        slots_kernel,
        grid=(D // tile,),
        out_shape=jax.ShapeDtypeStruct((slots, D), BF),
        in_specs=[pl.BlockSpec((slots, tokens), lambda j: (0, 0))]
        + [pl.BlockSpec((tokens, tile), lambda j: (0, j))] * len(blocks),
        out_specs=pl.BlockSpec((slots, tile), lambda j: (0, j)),
        compiler_params=pltpu.CompilerParams(vmem_limit_bytes=VMEM),
        cost_estimate=pl.CostEstimate(flops=slots, bytes_accessed=slots, transcendentals=0),
        name="slots",
    )(place, *blocks)


def together(*values):
    return lax.optimization_barrier(values)


def tuned_device(
    hidden,
    queries,
    new_keys,
    new_values,
    cache_keys,
    cache_values,
    out_weight,
    norm_gain,
    gate_proj,
    up_proj,
    down_proj,
    expert_ids,
    gate_fixed,
):
    y, c, z, x = (lax.axis_index(axis) for axis in AXES)
    tokens = hidden.shape[1]
    group = queries.shape[2] // HD // KVH
    source = jnp.array(SOURCES, jnp.int32)[z]
    inner = (z == 1) | (z == 2)

    def by_head(value):
        return value[0].reshape(tokens, KVH, -1).transpose(1, 0, 2)

    message = jnp.concatenate(
        [by_head(v) for v in (queries, cache_keys, new_keys, cache_values, new_values)], axis=-1
    )
    message = lax.all_to_all(message, ("y", "c"), split_axis=0, concat_axis=0, tiled=True)
    attended = attention(message, group)

    heads = [source[k] * 2 + x for k in range(4)] + [source[k] * 2 + (1 - x) for k in range(4)]
    in_order = jnp.concatenate(
        [lax.dynamic_slice_in_dim(attended, h * HD, HD, axis=1) for h in heads], axis=1
    )
    own = out_weight
    near, middle_in, across = together(along(own, OUTER), along(own, INNER), swap(own, "x"))
    middle_out, far_in, near_x, ids, gates = together(
        along(middle_in, OUTWARD),
        along(near, INNER),
        swap(near, "x"),
        expert_ids[0],
        gate_fixed[0],
    )
    middle = jnp.where(inner, middle_in, middle_out)
    parts = 2
    width = D // parts
    columns = [slice(part * width, (part + 1) * width) for part in range(parts)]
    far_out, middle_x, last_in = together(
        along(far_in, OUTWARD), swap(middle, "x"), along(near_x[:, columns[1]], INNER)
    )
    places, shares = routing(ids, gates, z, inner)
    far = jnp.where(inner, far_in, far_out)
    line = [own, near, middle, far, across, near_x, middle_x]
    last, last_out = together(swap(far[:, columns[0]], "x"), along(last_in, OUTWARD))
    last = [last, jnp.where(inner, last_in, last_out)]
    projected = []
    for part in range(parts):
        weight = jnp.concatenate([block[:, columns[part]] for block in line] + [last[part]], axis=0)
        partial = jnp.dot(in_order, weight, preferred_element_type=F32)
        partial = partial.reshape(2, 2, tokens, width)
        other = lax.dynamic_index_in_dim(partial, 1 - c, 1, keepdims=False).astype(BF)
        both = lax.dynamic_index_in_dim(partial, c, 1, keepdims=False) + swap(other, "c").astype(F32)
        other = lax.dynamic_index_in_dim(both, 1 - y, 0, keepdims=False).astype(BF)
        own = lax.dynamic_index_in_dim(both, y, 0, keepdims=False)
        projected.append(own + swap(other, "y").astype(F32))
    after_attention = (
        hidden[0].astype(F32) + jnp.concatenate(projected, axis=1)
    ).astype(BF)
    after_float = after_attention.astype(F32)
    normed = (
        after_float
        * lax.rsqrt(jnp.mean(after_float * after_float, axis=-1, keepdims=True) + 1e-06)
        * norm_gain.astype(F32)
    ).astype(BF)

    weights = (gate_proj, up_proj, down_proj)

    near, middle_in = along(normed, OUTER), along(normed, INNER)
    own_rows = plane_exchange(slots_of(places[0], normed))
    near_slots, own_rows = together(slots_of(places[1], near), own_rows)
    near_rows = plane_exchange(near_slots)
    middle_out, far_in = along(middle_in, OUTWARD), along(near, INNER)
    middle_slots, near_rows, far_in, shares = together(
        slots_of(places[2], middle_in, middle_out), near_rows, far_in, shares
    )
    middle_rows = plane_exchange(middle_slots)
    far_out = along(far_in, OUTWARD)
    own_out, near_out = experts((own_rows, near_rows), *weights)
    far_slots, middle_rows, own_out, near_out = together(
        slots_of(places[3], far_in, far_out), middle_rows, own_out, near_out
    )
    far_rows = plane_exchange(far_slots)
    middle_out = expert(middle_rows, *weights)
    far_rows, middle_out = together(far_rows, middle_out)
    far_out = expert(far_rows, *weights)

    far = plane_exchange(far_out)
    far_sum = combine(shares[3], far)
    middle_out, far, far_sum = together(middle_out, far, far_sum)
    middle = plane_exchange(middle_out)
    outer_far = along(far_sum, INWARD)
    near_out, middle, outer_far = together(near_out, middle, outer_far)
    near = plane_exchange(near_out)
    outer_middle = along(combine(shares[2], middle), INWARD)
    inner_far = along(combine(shares[3], far, outer_far), INNER)
    own_out, near, outer_middle, inner_far = together(own_out, near, outer_middle, inner_far)
    own = plane_exchange(own_out)
    inner_middle = along(combine(shares[2], middle, outer_middle), INNER)
    all_near = along(combine(shares[1], near, inner_far), OUTER)
    layer_output = combine(
        shares[0], own, after_attention, inner_middle, all_near
    )
    return (after_attention[None], layer_output[None])


def solution(mesh):
    sizes = (mesh.shape["ctx"], mesh.shape["exp"])
    if sizes == (4, 8):
        inner = Mesh(mesh.devices.reshape(2, 2, 4, 2), AXES)
        ctx, exp = ("y", "c"), ("z", "x")
        body = tuned_device
    else:
        inner, ctx, exp, body = mesh, "ctx", "exp", general_device
    both = (*AXES,) if body is tuned_device else ("ctx", "exp")
    token = P(exp, ctx, None)
    expert = P(both, None, None)
    return jax.shard_map(
        body,
        mesh=inner,
        in_specs=(
            token,
            token,
            token,
            token,
            token,
            token,
            P(both, None),
            P(),
            expert,
            expert,
            expert,
            token,
            token,
        ),
        out_specs=(token, token),
        check_vma=False,
    )
```

```python
import functools
import math

import jax
import jax.numpy as jnp
from jax import lax
from jax.experimental import pallas as pl
from jax.experimental.pallas import tpu as pltpu
from jax.sharding import Mesh
from jax.sharding import PartitionSpec as P

D = 4096
KVH = 4
HD = 128
TOPK = 4
AXES = ("y", "c", "z", "x")
PLANE = ("y", "c", "x")
BF = jnp.bfloat16
COST = 30 * 10**9
VMEM = 20 * 2**20
F32 = jnp.float32


def widen_heads(tensor, copies):
    row_count = tensor.shape[0]
    heads = tensor.reshape(row_count, KVH, HD)
    return jnp.repeat(heads, copies, axis=1).reshape(row_count, KVH * copies * HD)


def expert_ffn(incoming, gate_matrix, up_matrix, down_matrix):
    shape_in = incoming.shape
    flat_rows = incoming.reshape(-1, shape_in[-1])
    gate_act = jnp.dot(flat_rows, gate_matrix, preferred_element_type=jnp.float32)
    up_act = jnp.dot(flat_rows, up_matrix, preferred_element_type=jnp.float32)
    product = (jax.nn.silu(gate_act) * up_act).astype(jnp.bfloat16)
    output = jnp.dot(product, down_matrix, preferred_element_type=jnp.float32)
    return output.astype(jnp.bfloat16).reshape(shape_in)


def general_device(
    hidden,
    queries,
    new_keys,
    new_values,
    cache_keys,
    cache_values,
    out_weight,
    norm_gain,
    gate_proj,
    up_proj,
    down_proj,
    expert_ids,
    gate_fixed,
):
    context = lax.axis_size("ctx")
    experts_all = context * lax.axis_size("exp")
    tok_rows = hidden.shape[1]
    copies = context // KVH
    local_queries = queries[0]
    query_part, key_new, value_new, key_old, value_old = (
        lax.all_to_all(local_queries, "ctx", split_axis=1, concat_axis=0, tiled=True),
        lax.all_to_all(
            widen_heads(new_keys[0], copies), "ctx", split_axis=1, concat_axis=0, tiled=True
        ),
        lax.all_to_all(
            widen_heads(new_values[0], copies), "ctx", split_axis=1, concat_axis=0, tiled=True
        ),
        lax.all_to_all(
            widen_heads(cache_keys[0], copies), "ctx", split_axis=1, concat_axis=0, tiled=True
        ),
        lax.all_to_all(
            widen_heads(cache_values[0], copies), "ctx", split_axis=1, concat_axis=0, tiled=True
        ),
    )
    key_rows = jnp.concatenate([key_old, key_new], axis=0)
    value_rows = jnp.concatenate([value_old, value_new], axis=0)
    window = query_part.shape[0]
    heads_here = query_part.shape[1] // HD
    total_cache = key_old.shape[0]
    block_rows = min(512, window)
    block_count = window // block_rows
    key_pos = jnp.arange(key_rows.shape[0])

    def attend(operands):
        query_block, block_start = operands
        query_heads = query_block.reshape(block_rows, heads_here, HD)
        scores = jnp.einsum(
            "whd,ld->hwl", query_heads, key_rows, preferred_element_type=jnp.float32
        ) / math.sqrt(HD)
        query_pos = total_cache + block_start + jnp.arange(block_rows)
        scores = jnp.where(key_pos[None, None, :] <= query_pos[None, :, None], scores, -jnp.inf)
        highest = jnp.max(scores, axis=-1, keepdims=True)
        powers = jnp.exp(scores - highest)
        weights = (powers / jnp.sum(powers, axis=-1, keepdims=True)).astype(jnp.bfloat16)
        attended_block = jnp.einsum(
            "hwl,ld->whd", weights, value_rows, preferred_element_type=jnp.float32
        )
        return attended_block.astype(jnp.bfloat16).reshape(block_rows, heads_here * HD)

    attended = lax.map(
        attend,
        (
            query_part.reshape(block_count, block_rows, heads_here * HD),
            jnp.arange(block_count) * block_rows,
        ),
    ).reshape(window, heads_here * HD)
    proj_rows = lax.all_gather(out_weight, "exp", axis=0, tiled=True)
    projected = lax.psum_scatter(
        jnp.dot(attended, proj_rows, preferred_element_type=jnp.float32).astype(jnp.bfloat16),
        "ctx",
        scatter_dimension=0,
        tiled=True,
    ).astype(jnp.float32)
    after_attention = (hidden[0].astype(jnp.float32) + projected).astype(jnp.bfloat16)
    after_float = after_attention.astype(jnp.float32)
    normed = (
        after_float
        * lax.rsqrt(jnp.mean(after_float * after_float, axis=-1, keepdims=True) + 1e-06)
        * norm_gain.astype(jnp.float32)
    ).astype(jnp.bfloat16)
    capacity = max(2, 2 * tok_rows * TOPK // experts_all)
    flat_ids = expert_ids[0].reshape(-1)
    one_hot = (flat_ids[:, None] == jnp.arange(experts_all, dtype=jnp.int32)[None, :]).astype(
        jnp.int32
    )
    earlier = jnp.cumsum(one_hot, axis=0) - one_hot
    slot_index = jnp.sum(earlier * one_hot, axis=1)
    target = flat_ids * capacity + slot_index
    sources = jnp.repeat(normed, TOPK, axis=0)
    outgoing = jnp.zeros((experts_all * capacity, D), jnp.bfloat16).at[target].set(sources)
    results = expert_ffn(
        lax.all_to_all(
            outgoing.reshape(experts_all, capacity, D),
            ("ctx", "exp"),
            split_axis=0,
            concat_axis=0,
            tiled=True,
        ),
        gate_proj[0],
        up_proj[0],
        down_proj[0],
    )
    returned = lax.all_to_all(results, ("ctx", "exp"), split_axis=0, concat_axis=0, tiled=True)
    back_rows = returned.reshape(experts_all * capacity, D)[target]
    shares = gate_fixed[0].astype(jnp.float32) / 65536.0
    expert_sum = jnp.sum(
        back_rows.astype(jnp.float32).reshape(tok_rows, TOPK, D) * shares[:, :, None], axis=1
    )
    layer_output = (after_float + expert_sum).astype(jnp.bfloat16)
    return (after_attention[None], layer_output[None])


def swap(value, axis):
    return lax.ppermute(value, axis, [(0, 1), (1, 0)])


def along(value, pairs):
    return lax.ppermute(value, "z", pairs)


OUTER = [(0, 1), (1, 0), (2, 3), (3, 2)]
INNER = [(1, 2), (2, 1)]
OUTWARD = [(1, 0), (2, 3)]
INWARD = [(0, 1), (3, 2)]

SOURCES = ((0, 1, 2, 3), (1, 0, 2, 3), (2, 3, 1, 0), (3, 2, 1, 0))


def along_z(own, inner):
    near, middle_in = along(own, OUTER), along(own, INNER)
    middle_out, far_in = along(middle_in, OUTWARD), along(near, INNER)
    far_out = along(far_in, OUTWARD)
    return [own, near, jnp.where(inner, middle_in, middle_out), jnp.where(inner, far_in, far_out)]


def attend_kernel(message_ref, out_ref, keys, values, *, group, tokens):
    width = group * HD
    blocks = message_ref.shape[0]
    cached = blocks * tokens
    for s in range(blocks):
        rows = pl.ds(s * tokens, tokens)
        later = pl.ds(cached + s * tokens, tokens)
        keys[rows, :] = message_ref[s, :, width : width + HD]
        keys[later, :] = message_ref[s, :, width + HD : width + 2 * HD]
        values[rows, :] = message_ref[s, :, width + 2 * HD : width + 3 * HD]
        values[later, :] = message_ref[s, :, width + 3 * HD : width + 4 * HD]
    factor = math.log2(math.e) / math.sqrt(HD)
    row = lax.broadcasted_iota(jnp.int32, (tokens, tokens), 0)
    column = lax.broadcasted_iota(jnp.int32, (tokens, tokens), 1)
    allowed = jnp.concatenate([column <= row] * 2, axis=0)
    for s in range(blocks):
        before = cached + s * tokens

        def two_heads(step, carry):
            first = pl.multiple_of(step * 2 * HD, 2 * HD)
            second = pl.multiple_of(step * 2 * HD + HD, HD)
            queries = jnp.concatenate(
                [message_ref[s, :, pl.ds(first, HD)], message_ref[s, :, pl.ds(second, HD)]], axis=0
            )
            dims = (((1,), (1,)), ((), ()))
            old = lax.dot_general(
                queries, keys[:before, :], dims, preferred_element_type=F32
            )
            own = lax.dot_general(
                queries, keys[before : before + tokens, :], dims, preferred_element_type=F32
            )
            own = jnp.where(allowed, own, -jnp.inf)
            highest = jnp.maximum(
                jnp.max(old, axis=-1, keepdims=True), jnp.max(own, axis=-1, keepdims=True)
            )
            old = jnp.exp2((old - highest) * factor)
            own = jnp.exp2((own - highest) * factor)
            total = jnp.sum(old, axis=-1, keepdims=True) + jnp.sum(own, axis=-1, keepdims=True)
            mixed = jnp.dot(old.astype(BF), values[:before, :], preferred_element_type=F32)
            mixed += jnp.dot(
                own.astype(BF), values[before : before + tokens, :], preferred_element_type=F32
            )
            mixed = (mixed / total).astype(BF)
            out_ref[pl.ds(s * tokens, tokens), pl.ds(first, HD)] = mixed[:tokens]
            out_ref[pl.ds(s * tokens, tokens), pl.ds(second, HD)] = mixed[tokens:]
            return carry

        lax.fori_loop(0, group // 2, two_heads, 0)


def attention(message, group):
    blocks, tokens, _ = message.shape
    window = blocks * tokens
    live = blocks * tokens + tokens * (blocks + 1) // 2
    return pl.pallas_call(
        functools.partial(attend_kernel, group=group, tokens=tokens),
        out_shape=jax.ShapeDtypeStruct((window, group * HD), BF),
        in_specs=[pl.BlockSpec(memory_space=pltpu.VMEM)],
        out_specs=pl.BlockSpec(memory_space=pltpu.VMEM),
        scratch_shapes=[pltpu.VMEM((2 * window, HD), BF), pltpu.VMEM((2 * window, HD), BF)],
        compiler_params=pltpu.CompilerParams(vmem_limit_bytes=32 * 2**20),
        cost_estimate=pl.CostEstimate(
            flops=4 * window * group * HD * live,
            bytes_accessed=2 * message.size + 2 * window * group * HD,
            transcendentals=window * group * live,
        ),
        name="attention",
    )(message)


def routing(ids, gates, z, inner):
    tokens = ids.shape[0]
    plane = 8
    both = along_z(jnp.concatenate([ids, gates], axis=1), inner)
    both = jnp.stack(both)
    ids4, gates4 = both[..., :TOPK], both[..., TOPK:]
    place = jnp.arange(plane)
    y, c, x = place // 4, place // 2 % 2, place % 2
    experts = (y * 2 + c) * 8 + z * 2 + x
    capacity = max(2, 2 * tokens * TOPK // 32)
    same = ids4[:, None] == experts[None, :, None, None]
    chosen = same.any(-1)
    gate = jnp.sum(jnp.where(same, gates4[:, None], 0), axis=-1)
    earlier = (jnp.arange(tokens)[:, None] < jnp.arange(tokens)[None, :]).astype(BF)
    rank = jnp.dot(
        chosen.astype(BF).reshape(4 * plane, tokens), earlier, preferred_element_type=F32
    )
    rank = rank.reshape(4, plane, 1, tokens).astype(jnp.int32)
    at_slot = chosen[:, :, None, :] & (rank == jnp.arange(capacity)[None, None, :, None])
    high = (gate >> 8).astype(F32) / 256.0
    low = (gate & 255).astype(F32) / 65536.0
    slots = plane * capacity

    def spread(part):
        return jnp.where(at_slot, part[:, :, None, :], 0.0).astype(BF).reshape(4, slots, tokens)

    places = at_slot.astype(BF).reshape(4, slots, tokens)
    shares = jnp.concatenate([spread(high), spread(low)], axis=-1).transpose(0, 2, 1)
    return places, shares


def plane_exchange(rows):
    blocks = rows.reshape(8, -1, D)
    return lax.all_to_all(blocks, PLANE, split_axis=0, concat_axis=0, tiled=True).reshape(-1, D)


def experts_kernel(*refs, blocks, steps):
    rows, (gate_ref, up_ref, down_ref) = refs[:blocks], refs[blocks : blocks + 3]
    outs, (gate, up, product) = refs[blocks + 3 : 2 * blocks + 3], refs[2 * blocks + 3 :]
    step = pl.program_id(0)
    count = rows[0].shape[0]
    spans = [pl.ds(block * count, count) for block in range(blocks)]

    @pl.when(step < steps)
    def _():
        for ref, span in zip(rows, spans):
            more_gate = jnp.dot(ref[...], gate_ref[0], preferred_element_type=F32)
            more_up = jnp.dot(ref[...], up_ref[0], preferred_element_type=F32)

            @pl.when(step == 0)
            def _():
                gate[span, :] = more_gate
                up[span, :] = more_up

            @pl.when((step > 0) & (step < steps - 1))
            def _():
                gate[span, :] += more_gate
                up[span, :] += more_up

            @pl.when(step == steps - 1)
            def _():
                total = gate[span, :] + more_gate
                silu = total / (1.0 + jnp.exp(-total))
                product[span, :] = (silu * (up[span, :] + more_up)).astype(BF)

    @pl.when(step >= steps)
    def _():
        for ref, span in zip(outs, spans):
            ref[...] = jnp.dot(
                product[span, :], down_ref[0], preferred_element_type=F32
            ).astype(BF)


def experts(blocks, gate_proj, up_proj, down_proj):
    count, hidden = blocks[0].shape[0], gate_proj.shape[2]
    total = count * len(blocks)
    steps = 4
    tile = D // steps
    read = pl.BlockSpec((count, tile), lambda j: (0, jnp.minimum(j, steps - 1)))
    write = pl.BlockSpec((count, tile), lambda j: (0, jnp.maximum(j - steps, 0)))
    inner = pl.BlockSpec((1, tile, hidden), lambda j: (0, jnp.minimum(j, steps - 1), 0))
    outer = pl.BlockSpec((1, hidden, tile), lambda j: (0, 0, jnp.maximum(j - steps, 0)))
    return pl.pallas_call(
        functools.partial(experts_kernel, blocks=len(blocks), steps=steps),
        grid=(2 * steps,),
        out_shape=[jax.ShapeDtypeStruct((count, D), BF)] * len(blocks),
        in_specs=[read] * len(blocks) + [inner, inner, outer],
        out_specs=[write] * len(blocks),
        scratch_shapes=[
            pltpu.VMEM((total, hidden), F32),
            pltpu.VMEM((total, hidden), F32),
            pltpu.VMEM((total, hidden), BF),
        ],
        compiler_params=pltpu.CompilerParams(vmem_limit_bytes=58 * 2**20),
        cost_estimate=pl.CostEstimate(
            flops=total, bytes_accessed=total, transcendentals=0
        ),
        name="experts",
    )(*blocks, gate_proj, up_proj, down_proj)


def expert_kernel(rows_ref, gate_ref, up_ref, down_ref, out_ref, total):
    step = pl.program_id(0)
    rows = rows_ref[...]
    gate = jnp.dot(rows, gate_ref[0], preferred_element_type=F32)
    up = jnp.dot(rows, up_ref[0], preferred_element_type=F32)
    product = (gate / (1.0 + jnp.exp(-gate)) * up).astype(BF)
    output = jnp.dot(product, down_ref[0], preferred_element_type=F32)

    @pl.when(step == 0)
    def _():
        total[...] = output

    @pl.when((step > 0) & (step < pl.num_programs(0) - 1))
    def _():
        total[...] += output

    @pl.when(step == pl.num_programs(0) - 1)
    def _():
        out_ref[...] = (total[...] + output).astype(BF)


def expert(rows, gate_proj, up_proj, down_proj):
    count, hidden = rows.shape[0], gate_proj.shape[2]
    tile = 256
    return pl.pallas_call(
        expert_kernel,
        grid=(hidden // tile,),
        out_shape=jax.ShapeDtypeStruct(rows.shape, BF),
        in_specs=[
            pl.BlockSpec((count, D), lambda j: (0, 0)),
            pl.BlockSpec((1, D, tile), lambda j: (0, 0, j)),
            pl.BlockSpec((1, D, tile), lambda j: (0, 0, j)),
            pl.BlockSpec((1, tile, D), lambda j: (0, j, 0)),
        ],
        out_specs=pl.BlockSpec((count, D), lambda j: (0, 0)),
        scratch_shapes=[pltpu.VMEM((count, D), F32)],
        compiler_params=pltpu.CompilerParams(vmem_limit_bytes=58 * 2**20),
        cost_estimate=pl.CostEstimate(
            flops=6 * count * D * hidden,
            bytes_accessed=6 * D * hidden + 4 * count * D,
            transcendentals=count * hidden,
        ),
        name="expert",
    )(rows, gate_proj, up_proj, down_proj)


def combine_kernel(share_ref, rows_ref, *refs):
    *added, out_ref = refs
    both = jnp.dot(share_ref[...], rows_ref[...], preferred_element_type=F32)
    tokens = out_ref.shape[0]
    total = both[:tokens] + both[tokens:]
    for ref in added:
        total += ref[...].astype(F32)
    out_ref[...] = total.astype(out_ref.dtype)


def combine(share, rows, *added):
    slots = rows.shape[0]
    tokens = share.shape[0] // 2
    tile = D // 2
    block = pl.BlockSpec((tokens, tile), lambda j: (0, j))
    return pl.pallas_call(
        combine_kernel,
        grid=(D // tile,),
        out_shape=jax.ShapeDtypeStruct((tokens, D), BF),
        in_specs=[
            pl.BlockSpec((2 * tokens, slots), lambda j: (0, 0)),
            pl.BlockSpec((slots, tile), lambda j: (0, j)),
        ]
        + [block] * len(added),
        out_specs=block,
        compiler_params=pltpu.CompilerParams(vmem_limit_bytes=VMEM),
        cost_estimate=pl.CostEstimate(
            flops=tokens, bytes_accessed=tokens, transcendentals=0
        ),
        name="combine",
    )(share, rows, *added)


def slots_kernel(place_ref, *refs):
    *blocks, out_ref = refs
    block = blocks[0][...]
    for ref in blocks[1:]:
        block = block + ref[...]
    out_ref[...] = jnp.dot(place_ref[...], block, preferred_element_type=F32).astype(BF)


def slots_of(place, *blocks, cost=None):
    slots, tokens = place.shape
    tile = D // 2
    return pl.pallas_call(
        slots_kernel,
        grid=(D // tile,),
        out_shape=jax.ShapeDtypeStruct((slots, D), BF),
        in_specs=[pl.BlockSpec((slots, tokens), lambda j: (0, 0))]
        + [pl.BlockSpec((tokens, tile), lambda j: (0, j))] * len(blocks),
        out_specs=pl.BlockSpec((slots, tile), lambda j: (0, j)),
        compiler_params=pltpu.CompilerParams(vmem_limit_bytes=VMEM),
        cost_estimate=pl.CostEstimate(
            flops=cost or slots, bytes_accessed=slots, transcendentals=0
        ),
        name="slots",
    )(place, *blocks)


def together(*values):
    return lax.optimization_barrier(values)


def tuned_device(
    hidden,
    queries,
    new_keys,
    new_values,
    cache_keys,
    cache_values,
    out_weight,
    norm_gain,
    gate_proj,
    up_proj,
    down_proj,
    expert_ids,
    gate_fixed,
):
    y, c, z, x = (lax.axis_index(axis) for axis in AXES)
    tokens = hidden.shape[1]
    group = queries.shape[2] // HD // KVH
    source = jnp.array(SOURCES, jnp.int32)[z]
    inner = (z == 1) | (z == 2)

    def by_head(value):
        return value[0].reshape(tokens, KVH, -1).transpose(1, 0, 2)

    message = jnp.concatenate(
        [by_head(v) for v in (queries, cache_keys, new_keys, cache_values, new_values)], axis=-1
    )
    message = lax.all_to_all(message, ("y", "c"), split_axis=0, concat_axis=0, tiled=True)
    attended = attention(message, group)

    heads = [source[k] * 2 + x for k in range(4)] + [source[k] * 2 + (1 - x) for k in range(4)]
    in_order = jnp.concatenate(
        [lax.dynamic_slice_in_dim(attended, h * HD, HD, axis=1) for h in heads], axis=1
    )
    own = out_weight
    near, middle_in, across = together(along(own, OUTER), along(own, INNER), swap(own, "x"))
    middle_out, far_in, near_x, ids, gates = together(
        along(middle_in, OUTWARD),
        along(near, INNER),
        swap(near, "x"),
        expert_ids[0],
        gate_fixed[0],
    )
    middle = jnp.where(inner, middle_in, middle_out)
    parts = 2
    width = D // parts
    columns = [slice(part * width, (part + 1) * width) for part in range(parts)]
    first = jnp.concatenate([own, near, middle, across, near_x], axis=0)
    early_heads = jnp.concatenate([in_order[:, : 3 * HD], in_order[:, 4 * HD : 6 * HD]], axis=1)
    late_heads = jnp.concatenate([in_order[:, 3 * HD : 4 * HD], in_order[:, 6 * HD :]], axis=1)
    early = [
        jnp.dot(early_heads, first[:, at], preferred_element_type=F32) for at in columns
    ]
    far_out, middle_x, last_in, *early = together(
        along(far_in, OUTWARD), swap(middle, "x"), along(near_x[:, columns[1]], INNER), *early
    )
    places, shares = routing(ids, gates, z, inner)
    far = jnp.where(inner, far_in, far_out)
    late = [far, middle_x]
    last, last_out = together(swap(far[:, columns[0]], "x"), along(last_in, OUTWARD))
    last = [last, jnp.where(inner, last_in, last_out)]
    projected = []
    for part in range(parts):
        weight = jnp.concatenate([block[:, columns[part]] for block in late] + [last[part]], axis=0)
        partial = early[part] + jnp.dot(late_heads, weight, preferred_element_type=F32)
        partial = partial.reshape(2, 2, tokens, width)
        other = lax.dynamic_index_in_dim(partial, 1 - c, 1, keepdims=False).astype(BF)
        both = lax.dynamic_index_in_dim(partial, c, 1, keepdims=False) + swap(other, "c").astype(F32)
        other = lax.dynamic_index_in_dim(both, 1 - y, 0, keepdims=False).astype(BF)
        own = lax.dynamic_index_in_dim(both, y, 0, keepdims=False)
        projected.append(own + swap(other, "y").astype(F32))
    after_attention = (
        hidden[0].astype(F32) + jnp.concatenate(projected, axis=1)
    ).astype(BF)
    after_float = after_attention.astype(F32)
    normed = (
        after_float
        * lax.rsqrt(jnp.mean(after_float * after_float, axis=-1, keepdims=True) + 1e-06)
        * norm_gain.astype(F32)
    ).astype(BF)

    weights = (gate_proj, up_proj, down_proj)

    near, middle_in = along(normed, OUTER), along(normed, INNER)
    own_rows = plane_exchange(slots_of(places[0], normed))
    near_slots, own_rows = together(slots_of(places[1], near, cost=COST), own_rows)
    near_rows = plane_exchange(near_slots)
    middle_out, far_in = along(middle_in, OUTWARD), along(near, INNER)
    middle_slots, near_rows, far_in, shares = together(
        slots_of(places[2], middle_in, middle_out, cost=COST), near_rows, far_in, shares
    )
    middle_rows = plane_exchange(middle_slots)
    far_out = along(far_in, OUTWARD)
    own_out, near_out = experts((own_rows, near_rows), *weights)
    far_slots, middle_rows, own_out, near_out = together(
        slots_of(places[3], far_in, far_out, cost=COST), middle_rows, own_out, near_out
    )
    far_rows = plane_exchange(far_slots)
    middle_out = expert(middle_rows, *weights)
    far_rows, middle_out = together(far_rows, middle_out)
    far_out = expert(far_rows, *weights)

    far = plane_exchange(far_out)
    far_sum = combine(shares[3], far)
    middle_out, far, far_sum = together(middle_out, far, far_sum)
    middle = plane_exchange(middle_out)
    outer_far = along(far_sum, INWARD)
    inner_sum = combine(shares[3], far, outer_far)
    near_out, middle, inner_sum = together(near_out, middle, inner_sum)
    near = plane_exchange(near_out)
    inner_far = along(inner_sum, INNER)
    outer_middle = along(combine(shares[2], middle), INWARD)
    near_sum = combine(shares[1], near, inner_far)
    own_out, near_sum = together(own_out, near_sum)
    own = plane_exchange(own_out)
    inner_middle = along(combine(shares[2], middle, outer_middle), INNER)
    all_near = along(near_sum, OUTER)
    layer_output = combine(
        shares[0], own, after_attention, inner_middle, all_near
    )
    return (after_attention[None], layer_output[None])


def solution(mesh):
    sizes = (mesh.shape["ctx"], mesh.shape["exp"])
    if sizes == (4, 8):
        inner = Mesh(mesh.devices.reshape(2, 2, 4, 2), AXES)
        ctx, exp = ("y", "c"), ("z", "x")
        body = tuned_device
    else:
        inner, ctx, exp, body = mesh, "ctx", "exp", general_device
    both = (*AXES,) if body is tuned_device else ("ctx", "exp")
    token = P(exp, ctx, None)
    expert = P(both, None, None)
    return jax.shard_map(
        body,
        mesh=inner,
        in_specs=(
            token,
            token,
            token,
            token,
            token,
            token,
            P(both, None),
            P(),
            expert,
            expert,
            expert,
            token,
            token,
        ),
        out_specs=(token, token),
        check_vma=False,
    )
```

```python
import functools
import math

import jax
import jax.numpy as jnp
from jax import lax
from jax.experimental import pallas as pl
from jax.experimental.pallas import tpu as pltpu
from jax.sharding import Mesh
from jax.sharding import PartitionSpec as P

D = 4096
KVH = 4
HD = 128
TOPK = 4
AXES = ("y", "c", "z", "x")
PLANE = ("y", "c", "x")
BF = jnp.bfloat16
COST = 30 * 10**9
VMEM = 20 * 2**20
F32 = jnp.float32


def widen_heads(tensor, copies):
    row_count = tensor.shape[0]
    heads = tensor.reshape(row_count, KVH, HD)
    return jnp.repeat(heads, copies, axis=1).reshape(row_count, KVH * copies * HD)


def expert_ffn(incoming, gate_matrix, up_matrix, down_matrix):
    shape_in = incoming.shape
    flat_rows = incoming.reshape(-1, shape_in[-1])
    gate_act = jnp.dot(flat_rows, gate_matrix, preferred_element_type=jnp.float32)
    up_act = jnp.dot(flat_rows, up_matrix, preferred_element_type=jnp.float32)
    product = (jax.nn.silu(gate_act) * up_act).astype(jnp.bfloat16)
    output = jnp.dot(product, down_matrix, preferred_element_type=jnp.float32)
    return output.astype(jnp.bfloat16).reshape(shape_in)


def general_device(
    hidden,
    queries,
    new_keys,
    new_values,
    cache_keys,
    cache_values,
    out_weight,
    norm_gain,
    gate_proj,
    up_proj,
    down_proj,
    expert_ids,
    gate_fixed,
):
    context = lax.axis_size("ctx")
    experts_all = context * lax.axis_size("exp")
    tok_rows = hidden.shape[1]
    copies = context // KVH
    local_queries = queries[0]
    query_part, key_new, value_new, key_old, value_old = (
        lax.all_to_all(local_queries, "ctx", split_axis=1, concat_axis=0, tiled=True),
        lax.all_to_all(
            widen_heads(new_keys[0], copies), "ctx", split_axis=1, concat_axis=0, tiled=True
        ),
        lax.all_to_all(
            widen_heads(new_values[0], copies), "ctx", split_axis=1, concat_axis=0, tiled=True
        ),
        lax.all_to_all(
            widen_heads(cache_keys[0], copies), "ctx", split_axis=1, concat_axis=0, tiled=True
        ),
        lax.all_to_all(
            widen_heads(cache_values[0], copies), "ctx", split_axis=1, concat_axis=0, tiled=True
        ),
    )
    key_rows = jnp.concatenate([key_old, key_new], axis=0)
    value_rows = jnp.concatenate([value_old, value_new], axis=0)
    window = query_part.shape[0]
    heads_here = query_part.shape[1] // HD
    total_cache = key_old.shape[0]
    block_rows = min(512, window)
    block_count = window // block_rows
    key_pos = jnp.arange(key_rows.shape[0])

    def attend(operands):
        query_block, block_start = operands
        query_heads = query_block.reshape(block_rows, heads_here, HD)
        scores = jnp.einsum(
            "whd,ld->hwl", query_heads, key_rows, preferred_element_type=jnp.float32
        ) / math.sqrt(HD)
        query_pos = total_cache + block_start + jnp.arange(block_rows)
        scores = jnp.where(key_pos[None, None, :] <= query_pos[None, :, None], scores, -jnp.inf)
        highest = jnp.max(scores, axis=-1, keepdims=True)
        powers = jnp.exp(scores - highest)
        weights = (powers / jnp.sum(powers, axis=-1, keepdims=True)).astype(jnp.bfloat16)
        attended_block = jnp.einsum(
            "hwl,ld->whd", weights, value_rows, preferred_element_type=jnp.float32
        )
        return attended_block.astype(jnp.bfloat16).reshape(block_rows, heads_here * HD)

    attended = lax.map(
        attend,
        (
            query_part.reshape(block_count, block_rows, heads_here * HD),
            jnp.arange(block_count) * block_rows,
        ),
    ).reshape(window, heads_here * HD)
    proj_rows = lax.all_gather(out_weight, "exp", axis=0, tiled=True)
    projected = lax.psum_scatter(
        jnp.dot(attended, proj_rows, preferred_element_type=jnp.float32).astype(jnp.bfloat16),
        "ctx",
        scatter_dimension=0,
        tiled=True,
    ).astype(jnp.float32)
    after_attention = (hidden[0].astype(jnp.float32) + projected).astype(jnp.bfloat16)
    after_float = after_attention.astype(jnp.float32)
    normed = (
        after_float
        * lax.rsqrt(jnp.mean(after_float * after_float, axis=-1, keepdims=True) + 1e-06)
        * norm_gain.astype(jnp.float32)
    ).astype(jnp.bfloat16)
    capacity = max(2, 2 * tok_rows * TOPK // experts_all)
    flat_ids = expert_ids[0].reshape(-1)
    one_hot = (flat_ids[:, None] == jnp.arange(experts_all, dtype=jnp.int32)[None, :]).astype(
        jnp.int32
    )
    earlier = jnp.cumsum(one_hot, axis=0) - one_hot
    slot_index = jnp.sum(earlier * one_hot, axis=1)
    target = flat_ids * capacity + slot_index
    sources = jnp.repeat(normed, TOPK, axis=0)
    outgoing = jnp.zeros((experts_all * capacity, D), jnp.bfloat16).at[target].set(sources)
    results = expert_ffn(
        lax.all_to_all(
            outgoing.reshape(experts_all, capacity, D),
            ("ctx", "exp"),
            split_axis=0,
            concat_axis=0,
            tiled=True,
        ),
        gate_proj[0],
        up_proj[0],
        down_proj[0],
    )
    returned = lax.all_to_all(results, ("ctx", "exp"), split_axis=0, concat_axis=0, tiled=True)
    back_rows = returned.reshape(experts_all * capacity, D)[target]
    shares = gate_fixed[0].astype(jnp.float32) / 65536.0
    expert_sum = jnp.sum(
        back_rows.astype(jnp.float32).reshape(tok_rows, TOPK, D) * shares[:, :, None], axis=1
    )
    layer_output = (after_float + expert_sum).astype(jnp.bfloat16)
    return (after_attention[None], layer_output[None])


def swap(value, axis):
    return lax.ppermute(value, axis, [(0, 1), (1, 0)])


def along(value, pairs):
    return lax.ppermute(value, "z", pairs)


OUTER = [(0, 1), (1, 0), (2, 3), (3, 2)]
INNER = [(1, 2), (2, 1)]
OUTWARD = [(1, 0), (2, 3)]
INWARD = [(0, 1), (3, 2)]

SOURCES = ((0, 1, 2, 3), (1, 0, 2, 3), (2, 3, 1, 0), (3, 2, 1, 0))


def along_z(own, inner):
    near, middle_in = along(own, OUTER), along(own, INNER)
    middle_out, far_in = along(middle_in, OUTWARD), along(near, INNER)
    far_out = along(far_in, OUTWARD)
    return [own, near, jnp.where(inner, middle_in, middle_out), jnp.where(inner, far_in, far_out)]


def attend_kernel(message_ref, out_ref, keys, values, *, group, tokens):
    width = group * HD
    blocks = message_ref.shape[0]
    cached = blocks * tokens
    for s in range(blocks):
        rows = pl.ds(s * tokens, tokens)
        later = pl.ds(cached + s * tokens, tokens)
        keys[rows, :] = message_ref[s, :, width : width + HD]
        keys[later, :] = message_ref[s, :, width + HD : width + 2 * HD]
        values[rows, :] = message_ref[s, :, width + 2 * HD : width + 3 * HD]
        values[later, :] = message_ref[s, :, width + 3 * HD : width + 4 * HD]
    factor = math.log2(math.e) / math.sqrt(HD)
    row = lax.broadcasted_iota(jnp.int32, (tokens, tokens), 0)
    column = lax.broadcasted_iota(jnp.int32, (tokens, tokens), 1)
    allowed = jnp.concatenate([column <= row] * 2, axis=0)
    for s in range(blocks):
        before = cached + s * tokens

        def two_heads(step, carry):
            first = pl.multiple_of(step * 2 * HD, 2 * HD)
            second = pl.multiple_of(step * 2 * HD + HD, HD)
            queries = jnp.concatenate(
                [message_ref[s, :, pl.ds(first, HD)], message_ref[s, :, pl.ds(second, HD)]], axis=0
            )
            dims = (((1,), (1,)), ((), ()))
            old = lax.dot_general(
                queries, keys[:before, :], dims, preferred_element_type=F32
            )
            own = lax.dot_general(
                queries, keys[before : before + tokens, :], dims, preferred_element_type=F32
            )
            own = jnp.where(allowed, own, -jnp.inf)
            highest = jnp.maximum(
                jnp.max(old, axis=-1, keepdims=True), jnp.max(own, axis=-1, keepdims=True)
            )
            old = jnp.exp2((old - highest) * factor)
            own = jnp.exp2((own - highest) * factor)
            total = jnp.sum(old, axis=-1, keepdims=True) + jnp.sum(own, axis=-1, keepdims=True)
            mixed = jnp.dot(old.astype(BF), values[:before, :], preferred_element_type=F32)
            mixed += jnp.dot(
                own.astype(BF), values[before : before + tokens, :], preferred_element_type=F32
            )
            mixed = (mixed / total).astype(BF)
            out_ref[pl.ds(s * tokens, tokens), pl.ds(first, HD)] = mixed[:tokens]
            out_ref[pl.ds(s * tokens, tokens), pl.ds(second, HD)] = mixed[tokens:]
            return carry

        lax.fori_loop(0, group // 2, two_heads, 0)


def attention(message, group):
    blocks, tokens, _ = message.shape
    window = blocks * tokens
    live = blocks * tokens + tokens * (blocks + 1) // 2
    return pl.pallas_call(
        functools.partial(attend_kernel, group=group, tokens=tokens),
        out_shape=jax.ShapeDtypeStruct((window, group * HD), BF),
        in_specs=[pl.BlockSpec(memory_space=pltpu.VMEM)],
        out_specs=pl.BlockSpec(memory_space=pltpu.VMEM),
        scratch_shapes=[pltpu.VMEM((2 * window, HD), BF), pltpu.VMEM((2 * window, HD), BF)],
        compiler_params=pltpu.CompilerParams(vmem_limit_bytes=32 * 2**20),
        cost_estimate=pl.CostEstimate(
            flops=4 * window * group * HD * live,
            bytes_accessed=2 * message.size + 2 * window * group * HD,
            transcendentals=window * group * live,
        ),
        name="attention",
    )(message)


def routing(ids, gates, z, inner):
    tokens = ids.shape[0]
    plane = 8
    both = along_z(jnp.concatenate([ids, gates], axis=1), inner)
    both = jnp.stack(both)
    ids4, gates4 = both[..., :TOPK], both[..., TOPK:]
    place = jnp.arange(plane)
    y, c, x = place // 4, place // 2 % 2, place % 2
    experts = (y * 2 + c) * 8 + z * 2 + x
    capacity = max(2, 2 * tokens * TOPK // 32)
    same = ids4[:, None] == experts[None, :, None, None]
    chosen = same.any(-1)
    gate = jnp.sum(jnp.where(same, gates4[:, None], 0), axis=-1)
    earlier = (jnp.arange(tokens)[:, None] < jnp.arange(tokens)[None, :]).astype(BF)
    rank = jnp.dot(
        chosen.astype(BF).reshape(4 * plane, tokens), earlier, preferred_element_type=F32
    )
    rank = rank.reshape(4, plane, 1, tokens).astype(jnp.int32)
    at_slot = chosen[:, :, None, :] & (rank == jnp.arange(capacity)[None, None, :, None])
    high = (gate >> 8).astype(F32) / 256.0
    low = (gate & 255).astype(F32) / 65536.0
    slots = plane * capacity

    def spread(part):
        return jnp.where(at_slot, part[:, :, None, :], 0.0).astype(BF).reshape(4, slots, tokens)

    places = at_slot.astype(BF).reshape(4, slots, tokens)
    shares = jnp.concatenate([spread(high), spread(low)], axis=-1).transpose(0, 2, 1)
    return places, shares


def plane_exchange(rows):
    blocks = rows.reshape(8, -1, D)
    return lax.all_to_all(blocks, PLANE, split_axis=0, concat_axis=0, tiled=True).reshape(-1, D)


def experts_kernel(*refs, blocks, steps):
    rows, (gate_ref, up_ref, down_ref) = refs[:blocks], refs[blocks : blocks + 3]
    outs, (gate, up, product) = refs[blocks + 3 : 2 * blocks + 3], refs[2 * blocks + 3 :]
    step = pl.program_id(0)
    count = rows[0].shape[0]
    spans = [pl.ds(block * count, count) for block in range(blocks)]

    @pl.when(step < steps)
    def _():
        for ref, span in zip(rows, spans):
            more_gate = jnp.dot(ref[...], gate_ref[0], preferred_element_type=F32)
            more_up = jnp.dot(ref[...], up_ref[0], preferred_element_type=F32)

            @pl.when(step == 0)
            def _():
                gate[span, :] = more_gate
                up[span, :] = more_up

            @pl.when((step > 0) & (step < steps - 1))
            def _():
                gate[span, :] += more_gate
                up[span, :] += more_up

            @pl.when(step == steps - 1)
            def _():
                total = gate[span, :] + more_gate
                silu = total / (1.0 + jnp.exp(-total))
                product[span, :] = (silu * (up[span, :] + more_up)).astype(BF)

    @pl.when(step >= steps)
    def _():
        for ref, span in zip(outs, spans):
            ref[...] = jnp.dot(
                product[span, :], down_ref[0], preferred_element_type=F32
            ).astype(BF)


def experts(blocks, gate_proj, up_proj, down_proj):
    count, hidden = blocks[0].shape[0], gate_proj.shape[2]
    total = count * len(blocks)
    steps = 4
    tile = D // steps
    read = pl.BlockSpec((count, tile), lambda j: (0, jnp.minimum(j, steps - 1)))
    write = pl.BlockSpec((count, tile), lambda j: (0, jnp.maximum(j - steps, 0)))
    inner = pl.BlockSpec((1, tile, hidden), lambda j: (0, jnp.minimum(j, steps - 1), 0))
    outer = pl.BlockSpec((1, hidden, tile), lambda j: (0, 0, jnp.maximum(j - steps, 0)))
    return pl.pallas_call(
        functools.partial(experts_kernel, blocks=len(blocks), steps=steps),
        grid=(2 * steps,),
        out_shape=[jax.ShapeDtypeStruct((count, D), BF)] * len(blocks),
        in_specs=[read] * len(blocks) + [inner, inner, outer],
        out_specs=[write] * len(blocks),
        scratch_shapes=[
            pltpu.VMEM((total, hidden), F32),
            pltpu.VMEM((total, hidden), F32),
            pltpu.VMEM((total, hidden), BF),
        ],
        compiler_params=pltpu.CompilerParams(vmem_limit_bytes=58 * 2**20),
        cost_estimate=pl.CostEstimate(
            flops=total, bytes_accessed=total, transcendentals=0
        ),
        name="experts",
    )(*blocks, gate_proj, up_proj, down_proj)


def expert_kernel(rows_ref, gate_ref, up_ref, down_ref, out_ref, total):
    step = pl.program_id(0)
    rows = rows_ref[...]
    gate = jnp.dot(rows, gate_ref[0], preferred_element_type=F32)
    up = jnp.dot(rows, up_ref[0], preferred_element_type=F32)
    product = (gate / (1.0 + jnp.exp(-gate)) * up).astype(BF)
    output = jnp.dot(product, down_ref[0], preferred_element_type=F32)

    @pl.when(step == 0)
    def _():
        total[...] = output

    @pl.when((step > 0) & (step < pl.num_programs(0) - 1))
    def _():
        total[...] += output

    @pl.when(step == pl.num_programs(0) - 1)
    def _():
        out_ref[...] = (total[...] + output).astype(BF)


def expert(rows, gate_proj, up_proj, down_proj):
    count, hidden = rows.shape[0], gate_proj.shape[2]
    tile = 256
    return pl.pallas_call(
        expert_kernel,
        grid=(hidden // tile,),
        out_shape=jax.ShapeDtypeStruct(rows.shape, BF),
        in_specs=[
            pl.BlockSpec((count, D), lambda j: (0, 0)),
            pl.BlockSpec((1, D, tile), lambda j: (0, 0, j)),
            pl.BlockSpec((1, D, tile), lambda j: (0, 0, j)),
            pl.BlockSpec((1, tile, D), lambda j: (0, j, 0)),
        ],
        out_specs=pl.BlockSpec((count, D), lambda j: (0, 0)),
        scratch_shapes=[pltpu.VMEM((count, D), F32)],
        compiler_params=pltpu.CompilerParams(vmem_limit_bytes=58 * 2**20),
        cost_estimate=pl.CostEstimate(
            flops=6 * count * D * hidden,
            bytes_accessed=6 * D * hidden + 4 * count * D,
            transcendentals=count * hidden,
        ),
        name="expert",
    )(rows, gate_proj, up_proj, down_proj)


def combine_kernel(share_ref, rows_ref, *refs):
    *added, out_ref = refs
    both = jnp.dot(share_ref[...], rows_ref[...], preferred_element_type=F32)
    tokens = out_ref.shape[0]
    total = both[:tokens] + both[tokens:]
    for ref in added:
        total += ref[...].astype(F32)
    out_ref[...] = total.astype(out_ref.dtype)


def combine(share, rows, *added, cost=None, room=VMEM):
    slots = rows.shape[0]
    tokens = share.shape[0] // 2
    tile = D // 2
    block = pl.BlockSpec((tokens, tile), lambda j: (0, j))
    return pl.pallas_call(
        combine_kernel,
        grid=(D // tile,),
        out_shape=jax.ShapeDtypeStruct((tokens, D), BF),
        in_specs=[
            pl.BlockSpec((2 * tokens, slots), lambda j: (0, 0)),
            pl.BlockSpec((slots, tile), lambda j: (0, j)),
        ]
        + [block] * len(added),
        out_specs=block,
        compiler_params=pltpu.CompilerParams(vmem_limit_bytes=room),
        cost_estimate=pl.CostEstimate(
            flops=cost or tokens, bytes_accessed=tokens, transcendentals=0
        ),
        name="combine",
    )(share, rows, *added)


def slots_kernel(place_ref, *refs):
    *blocks, out_ref = refs
    block = blocks[0][...]
    for ref in blocks[1:]:
        block = block + ref[...]
    out_ref[...] = jnp.dot(place_ref[...], block, preferred_element_type=F32).astype(BF)


def slots_of(place, *blocks, cost=None):
    slots, tokens = place.shape
    tile = D // 2
    return pl.pallas_call(
        slots_kernel,
        grid=(D // tile,),
        out_shape=jax.ShapeDtypeStruct((slots, D), BF),
        in_specs=[pl.BlockSpec((slots, tokens), lambda j: (0, 0))]
        + [pl.BlockSpec((tokens, tile), lambda j: (0, j))] * len(blocks),
        out_specs=pl.BlockSpec((slots, tile), lambda j: (0, j)),
        compiler_params=pltpu.CompilerParams(vmem_limit_bytes=VMEM),
        cost_estimate=pl.CostEstimate(
            flops=cost or slots, bytes_accessed=slots, transcendentals=0
        ),
        name="slots",
    )(place, *blocks)


def together(*values):
    return lax.optimization_barrier(values)


def tuned_device(
    hidden,
    queries,
    new_keys,
    new_values,
    cache_keys,
    cache_values,
    out_weight,
    norm_gain,
    gate_proj,
    up_proj,
    down_proj,
    expert_ids,
    gate_fixed,
):
    y, c, z, x = (lax.axis_index(axis) for axis in AXES)
    tokens = hidden.shape[1]
    group = queries.shape[2] // HD // KVH
    source = jnp.array(SOURCES, jnp.int32)[z]
    inner = (z == 1) | (z == 2)

    def by_head(value):
        return value[0].reshape(tokens, KVH, -1).transpose(1, 0, 2)

    message = jnp.concatenate(
        [by_head(v) for v in (queries, cache_keys, new_keys, cache_values, new_values)], axis=-1
    )
    message = lax.all_to_all(message, ("y", "c"), split_axis=0, concat_axis=0, tiled=True)
    attended = attention(message, group)

    heads = [source[k] * 2 + x for k in range(4)] + [source[k] * 2 + (1 - x) for k in range(4)]
    in_order = jnp.concatenate(
        [lax.dynamic_slice_in_dim(attended, h * HD, HD, axis=1) for h in heads], axis=1
    )
    own = out_weight
    near, middle_in, across = together(along(own, OUTER), along(own, INNER), swap(own, "x"))
    middle_out, far_in, near_x, ids, gates = together(
        along(middle_in, OUTWARD),
        along(near, INNER),
        swap(near, "x"),
        expert_ids[0],
        gate_fixed[0],
    )
    middle = jnp.where(inner, middle_in, middle_out)
    parts = 2
    width = D // parts
    columns = [slice(part * width, (part + 1) * width) for part in range(parts)]
    first = jnp.concatenate([own, near, middle, across, near_x], axis=0)
    early_heads = jnp.concatenate([in_order[:, : 3 * HD], in_order[:, 4 * HD : 6 * HD]], axis=1)
    late_heads = jnp.concatenate([in_order[:, 3 * HD : 4 * HD], in_order[:, 6 * HD :]], axis=1)
    early = [
        jnp.dot(early_heads, first[:, at], preferred_element_type=F32) for at in columns
    ]
    far_out, middle_x, last_in, *early = together(
        along(far_in, OUTWARD), swap(middle, "x"), along(near_x[:, columns[1]], INNER), *early
    )
    places, shares = routing(ids, gates, z, inner)
    far = jnp.where(inner, far_in, far_out)
    late = [far, middle_x]
    last, last_out = together(swap(far[:, columns[0]], "x"), along(last_in, OUTWARD))
    last = [last, jnp.where(inner, last_in, last_out)]
    projected = []
    for part in range(parts):
        weight = jnp.concatenate([block[:, columns[part]] for block in late] + [last[part]], axis=0)
        partial = early[part] + jnp.dot(late_heads, weight, preferred_element_type=F32)
        partial = partial.reshape(2, 2, tokens, width)
        other = lax.dynamic_index_in_dim(partial, 1 - c, 1, keepdims=False).astype(BF)
        both = lax.dynamic_index_in_dim(partial, c, 1, keepdims=False) + swap(other, "c").astype(F32)
        other = lax.dynamic_index_in_dim(both, 1 - y, 0, keepdims=False).astype(BF)
        own = lax.dynamic_index_in_dim(both, y, 0, keepdims=False)
        projected.append(own + swap(other, "y").astype(F32))
    after_attention = (
        hidden[0].astype(F32) + jnp.concatenate(projected, axis=1)
    ).astype(BF)
    after_float = after_attention.astype(F32)
    normed = (
        after_float
        * lax.rsqrt(jnp.mean(after_float * after_float, axis=-1, keepdims=True) + 1e-06)
        * norm_gain.astype(F32)
    ).astype(BF)

    weights = (gate_proj, up_proj, down_proj)

    near, middle_in = along(normed, OUTER), along(normed, INNER)
    own_rows = plane_exchange(slots_of(places[0], normed))
    near_slots, own_rows = together(slots_of(places[1], near, cost=COST), own_rows)
    near_rows = plane_exchange(near_slots)
    middle_out, far_in = along(middle_in, OUTWARD), along(near, INNER)
    middle_slots, near_rows, far_in, shares = together(
        slots_of(places[2], middle_in, middle_out, cost=COST), near_rows, far_in, shares
    )
    middle_rows = plane_exchange(middle_slots)
    far_out = along(far_in, OUTWARD)
    own_out, near_out = experts((own_rows, near_rows), *weights)
    far_slots, middle_rows, own_out, near_out = together(
        slots_of(places[3], far_in, far_out, cost=COST), middle_rows, own_out, near_out
    )
    far_rows = plane_exchange(far_slots)
    middle_out = expert(middle_rows, *weights)
    far_rows, middle_out = together(far_rows, middle_out)
    far_out = expert(far_rows, *weights)

    far = plane_exchange(far_out)
    far_sum = combine(shares[3], far)
    middle_out, far, far_sum = together(middle_out, far, far_sum)
    middle = plane_exchange(middle_out)
    outer_far = along(far_sum, INWARD)
    near_out, middle, outer_far = together(near_out, middle, outer_far)
    near = plane_exchange(near_out)
    inner_far = along(combine(shares[3], far, outer_far), INNER)
    outer_middle = along(combine(shares[2], middle, cost=COST), INWARD)
    own_out, near = together(own_out, near)
    own = plane_exchange(own_out)
    all_near = along(combine(shares[1], near, inner_far), OUTER)
    inner_middle = along(combine(shares[2], middle, outer_middle, cost=COST), INNER)
    layer_output = combine(
        shares[0], own, after_attention, inner_middle, all_near, room=58 * 2**20
    )
    return (after_attention[None], layer_output[None])


def solution(mesh):
    sizes = (mesh.shape["ctx"], mesh.shape["exp"])
    if sizes == (4, 8):
        inner = Mesh(mesh.devices.reshape(2, 2, 4, 2), AXES)
        ctx, exp = ("y", "c"), ("z", "x")
        body = tuned_device
    else:
        inner, ctx, exp, body = mesh, "ctx", "exp", general_device
    both = (*AXES,) if body is tuned_device else ("ctx", "exp")
    token = P(exp, ctx, None)
    expert = P(both, None, None)
    return jax.shard_map(
        body,
        mesh=inner,
        in_specs=(
            token,
            token,
            token,
            token,
            token,
            token,
            P(both, None),
            P(),
            expert,
            expert,
            expert,
            token,
            token,
        ),
        out_specs=(token, token),
        check_vma=False,
    )
```
